32 devices in a mesh: seq: 8 (over z, x), dp: 4 (over y, core).
Axes of the slice: x: 2, y: 2, z: 4, core: 2. Of those that a mesh axis runs over, the one named last changes fastest.
Arguments:
- tokens: bfloat16 [4, 8192, 768], P('dp', 'seq'), may hold values from -8 to 8
- tile_mask: int32 [4, 8192], P('dp', 'seq'), may hold values from 0 to 1, as said below
- cotangent: bfloat16 [4, 8192, 768], P('dp', 'seq'), may hold values from -6 to 6
- qkv_weight: bfloat16 [768, 2304], replicated, may hold values from -0.21875 to 0.21875
- proj_weight: bfloat16 [768, 768], replicated, may hold values from -6 to 6
- proj_bias: bfloat16 [768], replicated, may hold values from -4 to 4
- up_weight: bfloat16 [768, 3072], replicated, may hold values from -0.21875 to 0.21875
- up_bias: bfloat16 [3072], replicated, may hold values from -4 to 4
- down_weight: bfloat16 [3072, 768], replicated, may hold values from -0.109375 to 0.109375
- down_bias: bfloat16 [768], replicated, may hold values from -4 to 4
- attn_gain: bfloat16 [768], replicated, may hold values from 0.5 to 1.5
- attn_shift: bfloat16 [768], replicated, may hold values from -4 to 4
- mlp_gain: bfloat16 [768], replicated, may hold values from 0.5 to 1.5
- mlp_shift: bfloat16 [768], replicated, may hold values from -4 to 4
- mask_vector: bfloat16 [768], replicated, may hold values from -5 to 5
Outputs:
- layer_out: bfloat16 [4, 8192, 768], P('dp', 'seq')
- tokens_grad: bfloat16 [4, 8192, 768], P('dp', 'seq')
- qkv_grad: float32 [768, 2304], P('seq')
- proj_grad: float32 [768, 768], P('seq')
- proj_bias_grad: float32 [768], P('seq')
- up_grad: float32 [768, 3072], P('seq')
- up_bias_grad: float32 [3072], P('seq')
- down_grad: float32 [3072, 768], P('seq')
- down_bias_grad: float32 [768], P('seq')
- attn_gain_grad: float32 [768], P('seq')
- attn_shift_grad: float32 [768], P('seq')
- mlp_gain_grad: float32 [768], P('seq')
- mlp_shift_grad: float32 [768], P('seq')
- mask_vector_grad: float32 [768], P('seq')
- stream_rms: float32 [3], replicated
The draws below stay inside these ranges and needn't reach their ends.
Inputs may be any that keep to these rules, and one draw needn't show every extreme that they name: `tile_mask`: in each slide the share of hidden tiles is drawn between a half and three quarters.
All inputs are finite; a program needn't handle non-finite values.
Results may differ from the reference program's by a relative error of at most 0.014.
Values may be sent and summed in bfloat16 or wider, within the bound.
No kernel may reach another device: no remote copies, remote signals or barrier semaphores. Data moves between devices by JAX's collectives and lax.ppermute only.
A program may use at most 320 MiB of HBM per device.

```python
import jax
import jax.numpy as jnp
from jax import lax

D = 768
HEADS = 16
HEAD_DIM = 48
FF = 3072
TOK_DEV = 1024
BRANCHES = 4
SLIDE = 8192
SLIDES = 4


def draw_tokens(key, part):
    key_base = jax.random.fold_in(jax.random.fold_in(key, 11), 0)
    position = jnp.arange(SLIDE, dtype=jnp.float32) / SLIDE
    ramp = 0.2 * (1.0 + 9.0 * position)
    values = jnp.clip(jax.random.normal(key_base, (SLIDES, SLIDE, D), jnp.float32), -4.0, 4.0)
    return (values * ramp[None, :, None]).astype(jnp.bfloat16)


def draw_tile_mask(key, part):
    key_share, key_tiles = jax.random.split(jax.random.fold_in(key, 23))
    share_limit = jax.random.randint(key_share, (SLIDES, 1), 2048, 3073)
    tile_draws = jax.random.randint(key_tiles, (SLIDES, SLIDE), 0, 4096)
    return (tile_draws < share_limit).astype(jnp.int32)


def block_scale(key, dims, cuts, low, high):
    loudness = 1.0
    for dim, shards_of in cuts:
        heights = jax.random.uniform(jax.random.fold_in(jax.random.fold_in(key, 6), dim), (shards_of,), jnp.float32, low / len(cuts), high / len(cuts))
        loudness = loudness * jnp.repeat(jnp.exp(heights), dims[dim] // shards_of).reshape((-1,) + (1,) * (len(dims) - 1 - dim))
    return loudness


def noise(key, dims, width, limit, shards=(), kind=jnp.bfloat16):
    values = width * jax.random.normal(key, dims, jnp.float32)
    if shards:
        values = values * block_scale(key, dims, shards, -0.22, 0.18)
    return jnp.clip(values, -limit, limit).astype(kind)


def setup_inputs(seed: int = 0) -> dict:
    keys = jax.random.split(jax.random.key(seed), 16)
    tokens = draw_tokens(jax.random.fold_in(keys[15], 71), 0)
    tile_mask = draw_tile_mask(jax.random.fold_in(keys[15], 71), 0)
    cotangent = noise(keys[2], (SLIDES, SLIDE, D), 1.0, 6.0, ((0, 4), (1, 8)))
    qkv_weight = noise(keys[3], (D, 3 * D), D ** -0.5, 0.21875)
    proj_weight = noise(keys[4], (D, D), 1 ** -0.5, 6.0)
    proj_bias = noise(keys[5], (D,), 0.3, 4.0)
    up_weight = noise(keys[6], (D, FF), D ** -0.5, 0.21875)
    up_bias = noise(keys[7], (FF,), 0.5, 4.0)
    down_weight = noise(keys[8], (FF, D), FF ** -0.5, 0.109375)
    down_bias = noise(keys[9], (D,), 0.3, 4.0)
    attn_gain = jnp.clip(1.0 + 0.1 * jax.random.normal(keys[10], (D,), jnp.float32), 0.5, 1.5).astype(jnp.bfloat16)
    attn_shift = noise(keys[11], (D,), 0.3, 4.0)
    mlp_gain = jnp.clip(1.0 + 0.1 * jax.random.normal(keys[12], (D,), jnp.float32), 0.5, 1.5).astype(jnp.bfloat16)
    mlp_shift = noise(keys[13], (D,), 0.3, 4.0)
    mask_vector = noise(keys[14], (D,), 1.0, 5.0)
    return {"tokens": tokens, "tile_mask": tile_mask, "cotangent": cotangent, "qkv_weight": qkv_weight, "proj_weight": proj_weight, "proj_bias": proj_bias, "up_weight": up_weight, "up_bias": up_bias, "down_weight": down_weight, "down_bias": down_bias, "attn_gain": attn_gain, "attn_shift": attn_shift, "mlp_gain": mlp_gain, "mlp_shift": mlp_shift, "mask_vector": mask_vector}


@jax.custom_vjp
def low(v):
    return lax.optimization_barrier(v.astype(jnp.bfloat16)).astype(jnp.float32)

@jax.custom_vjp
def low_back(v):
    return v

def low_keep(v):
    return (low(v), None)

def low_pass(kept, grad):
    return (grad,)

def back_keep(v):
    return (v, None)

def back_low(kept, grad):
    return (low(grad),)
low.defvjp(low_keep, low_pass)
low_back.defvjp(back_keep, back_low)
EPS = 1e-06
FILL = -1e+30

def layer_norm(inputs, scales, offsets):
    average = lax.optimization_barrier(jnp.mean(inputs, axis=-1, keepdims=True))
    centred = inputs - average
    spread = lax.optimization_barrier(jnp.mean(centred * centred, axis=-1, keepdims=True))
    return centred * lax.rsqrt(spread + EPS) * scales + offsets

def matmul(left_side, right_side):
    return jnp.dot(left_side, right_side, precision=lax.Precision.HIGHEST)

def attend_packed(triple):
    queries, key_rows, value_rows = triple
    scores = low_back(matmul(queries, key_rows.T) * HEAD_DIM ** (-0.5))
    totals = jax.nn.logsumexp(scores, axis=-1)
    probs = low(jnp.exp(scores - totals[:, None]))
    return (matmul(probs, value_rows), totals)

def to_units(field_in, dilation):
    segments = field_in.shape[0] // (TOK_DEV * dilation)
    last_count = field_in.shape[-1]
    shaped = field_in.reshape(segments, TOK_DEV, dilation, HEADS // dilation, dilation, last_count)
    diagonal = jnp.diagonal(shaped, axis1=2, axis2=4)
    ordered = jnp.transpose(diagonal, (0, 4, 2, 1, 3))
    return ordered.reshape(segments * HEADS, TOK_DEV, last_count)

def from_units(unit_rows, dilation, filler):
    last_count = unit_rows.shape[-1]
    segments = unit_rows.shape[0] // HEADS
    shaped = unit_rows.reshape(segments, dilation, HEADS // dilation, TOK_DEV, last_count)
    ordered = jnp.transpose(shaped, (0, 3, 1, 2, 4))
    select = jnp.eye(dilation, dtype=bool)[None, None, :, None, :, None]
    spread_out = jnp.where(select, ordered[:, :, :, :, None, :], filler)
    return spread_out.reshape(segments * TOK_DEV * dilation, HEADS, last_count)

def forward(tile_rows, hidden, qkv_weight, proj_weight, proj_bias, up_weight, up_bias, down_weight, down_bias, attn_gain, attn_shift, mlp_gain, mlp_shift, mask_vector):
    length = tile_rows.shape[0]
    start = jnp.where(hidden[:, None], mask_vector[None, :], tile_rows)
    normed = low(layer_norm(start, attn_gain, attn_shift))
    qkv = low_back(low(matmul(normed, qkv_weight)))
    split_qkv = qkv.reshape(length, 3, HEADS, HEAD_DIM)
    outputs = []
    totals_all = []
    for branch in range(BRANCHES):
        dilation = 2 ** branch
        triple = tuple((to_units(split_qkv[:, index], dilation) for index in range(3)))
        unit_out, unit_total = lax.map(jax.checkpoint(attend_packed), triple)
        unit_out = low_back(low(unit_out))
        outputs.append(from_units(unit_out, dilation, 0.0))
        totals_all.append(from_units(unit_total[..., None], dilation, FILL)[..., 0])
    stacked_totals = jnp.stack(totals_all)
    peak = lax.optimization_barrier(jnp.max(stacked_totals, axis=0))
    weights = jnp.exp(stacked_totals - peak)
    shares = weights / lax.optimization_barrier(jnp.sum(weights, axis=0))
    merged = lax.optimization_barrier(jnp.sum(shares[..., None] * jnp.stack(outputs), axis=0))
    attn = low(merged.reshape(length, D))
    middle = start + low_back(matmul(attn, proj_weight) + proj_bias)
    normed2 = low(layer_norm(middle, mlp_gain, mlp_shift))
    pre = low_back(matmul(normed2, up_weight) + up_bias)
    act = low(jax.nn.gelu(pre, approximate=False))
    final = middle + low_back(matmul(act, down_weight) + down_bias)
    visible = 1.0 - hidden.astype(jnp.float32)[:, None]
    sums = jnp.stack([jnp.sum(visible * tile_rows * tile_rows), jnp.sum(visible * middle * middle), jnp.sum(visible * final * final)])
    return (final, sums)

def reference(tokens, tile_mask, cotangent, qkv_weight, proj_weight, proj_bias, up_weight, up_bias, down_weight, down_bias, attn_gain, attn_shift, mlp_gain, mlp_shift, mask_vector):
    params = tuple((weight.astype(jnp.float32) for weight in (qkv_weight, proj_weight, proj_bias, up_weight, up_bias, down_weight, down_bias, attn_gain, attn_shift, mlp_gain, mlp_shift, mask_vector)))

    def slide_step(carry, inputs):
        tile_rows, mask_rows, cot_rows = inputs
        hidden = mask_rows == 1

        def apply(tile_values, *weights):
            return forward(tile_values, hidden, *weights)
        final, pullback, sums = jax.vjp(apply, tile_rows.astype(jnp.float32), *params, has_aux=True)
        grads = pullback(cot_rows.astype(jnp.float32))
        new_grads = tuple((total + grad for total, grad in zip(carry[0], grads[1:])))
        count = carry[2] + jnp.sum(1.0 - hidden.astype(jnp.float32))
        return ((new_grads, carry[1] + sums, count), (final.astype(jnp.bfloat16), grads[0].astype(jnp.bfloat16)))
    init = (tuple((jnp.zeros_like(weight) for weight in params)), jnp.zeros((3,), jnp.float32), jnp.zeros((), jnp.float32))
    (grads, sums, count), (layer_out, tokens_grad) = lax.scan(slide_step, init, (tokens, tile_mask, cotangent))
    stream_rms = jnp.sqrt(sums / (count * D))
    return (layer_out, tokens_grad, grads[0], grads[1], grads[2], grads[3], grads[4], grads[5], grads[6], grads[7], grads[8], grads[9], grads[10], grads[11], stream_rms)
```

```python
import numpy as np
import jax
import jax.numpy as jnp
from jax import lax
from jax.experimental import pallas as pl
from jax.experimental.pallas import tpu as pltpu
from jax.sharding import PartitionSpec as P

HEADS = 16
HD = 48
AUG = 64
TILES = 1024
EPS = 1e-06
FILL = -1e30
LN2 = float(np.log(2.0))
SCALE = HD**-0.5
QSCALE = SCALE / LN2
BF = jnp.bfloat16
F32 = jnp.float32


def nn(a, b):
    return lax.dot_general(a, b, (((1,), (0,)), ((), ())), preferred_element_type=F32)


def nt(a, b):
    return lax.dot_general(a, b, (((1,), (1,)), ((), ())), preferred_element_type=F32)


def tn(a, b):
    return lax.dot_general(a, b, (((0,), (0,)), ((), ())), preferred_element_type=F32)


GROUP = 8
GROUPS = HEADS // GROUP
D = HEADS * HD
ROWS = GROUP * HD
HALF, QUARTER, EIGHTH = TILES // 2, TILES // 4, TILES // 8
MIB = 1024 * 1024


def place_of(tile):
    return (tile & 1) * HALF + (tile >> 1 & 1) * QUARTER + (tile >> 2 & 1) * EIGHTH + (tile >> 3)


def order_matrix():
    tile = np.arange(TILES)
    matrix = np.zeros((TILES, TILES), np.float32)
    matrix[tile, place_of(tile)] = 1.0
    return jnp.asarray(matrix.astype(jnp.bfloat16))


def lanes2(h):
    return (h & 1) * HALF


def lanes4(h):
    return lanes2(h) + (h >> 1 & 1) * QUARTER


def rest2(h):
    return lanes2(h) + (1 - (h >> 1 & 1)) * QUARTER


def lanes8(h):
    return lanes4(h) + (h >> 2 & 1) * EIGHTH


def weight_tables(level, compact=False):
    count = TILES >> level
    classes = 8 >> level
    totals = {0: [2.0, 3.0, 4.0], 1: [2.0, 3.0], 2: [2.0]}[level]
    lane = np.arange(count)
    key_rows = np.zeros((classes, 16, count), np.float32)
    query_rows = np.zeros((classes, 16, count), np.float32)
    key_rows[:, 3:6] = 1.0
    for c in range(classes):
        inside = np.ones(count, bool)
        before = 1.0
        for i, total in enumerate(totals):
            bit = (lane >> (9 - level - i)) & 1
            wanted = 0 if compact and i == 0 else c >> i & 1
            inside = inside & (bit == wanted)
            step = np.log2(total) - np.log2(before)
            before = total
            high = np.float32(np.asarray(step, np.float32).astype(jnp.bfloat16))
            key_rows[c, 6 + 2 * i] = inside
            key_rows[c, 7 + 2 * i] = inside
            query_rows[c, 6 + 2 * i] = inside * high
            query_rows[c, 7 + 2 * i] = inside * (step - high)
    shape = (classes * 16, count)
    return (
        jnp.asarray(key_rows.reshape(shape).astype(jnp.bfloat16)),
        jnp.asarray(query_rows.reshape(shape).astype(jnp.bfloat16)),
    )


def value_rows(count):
    row = lax.broadcasted_iota(jnp.int32, (16, count), 0)
    return jnp.where(row < 3, 1.0, 0.0).astype(BF)


def stack(*parts):
    return jnp.concatenate(parts, axis=0)


def beside(*parts):
    return jnp.concatenate(parts, axis=1)


def head_rows(j, height=HD):
    return slice(j * height, (j + 1) * height)


def attend(keys, values, queries):
    scores = nn(keys, queries)
    peak = jnp.max(scores, axis=0, keepdims=True)
    probs = jnp.exp2(scores - peak).astype(BF)
    out = nn(values, probs)
    total = out[HD : HD + 1]
    return out[:HD] / total, peak + jnp.log2(total)


def split3(value):
    high = value.astype(BF).astype(F32)
    rest = value - high
    mid = rest.astype(BF).astype(F32)
    return high, mid, rest - mid


def split_rows(*values):
    row = lax.broadcasted_iota(jnp.int32, (16, values[0].shape[1]), 0)
    packed = jnp.zeros((16, values[0].shape[1]), F32)
    for i, value in enumerate(values):
        for k, piece in enumerate(split3(value)):
            packed = jnp.where(row == 3 * i + k, piece, packed)
    return packed


def column(row, width):
    turned = jnp.broadcast_to(row, (128, row.shape[1])).T
    return jnp.concatenate([turned] * (width // 128), axis=1)


def normalise(value):
    average = jnp.mean(value, axis=1, keepdims=True)
    centred = value - average
    spread = jnp.mean(centred * centred, axis=1, keepdims=True)
    scale = lax.rsqrt(spread + EPS)
    return centred * scale, scale


def embed_kernel(
    tok_ref, mask_ref, vec_ref, w_ref, order_ref,
    normed_ref, start_ref, square_ref, qkv_ref, q4_ref, q8_ref, kv4_ref, kvr_ref,
):
    step = pl.program_id(0)

    @pl.when(step == 0)
    def _():
        hidden = column(mask_ref[...].astype(F32), D) > 0.5
        rows = tok_ref[...].astype(F32)
        start = jnp.where(hidden, vec_ref[6:7], rows)
        start_ref[...] = start.astype(BF)
        squares = jnp.where(hidden, 0.0, rows * rows)
        square_ref[...] = jnp.broadcast_to(jnp.sum(squares, axis=0, keepdims=True), (8, D))
        normed = normalise(start)[0] * vec_ref[2:3] + vec_ref[3:4]
        normed_ref[...] = tn(normed.astype(BF), order_ref[...]).astype(BF)

    value = tn(w_ref[...], normed_ref[...])

    @pl.when(step < GROUPS)
    def _():
        low = (value * QSCALE).astype(BF)
        qkv_ref[...] = low
        for j in range(GROUP):
            rows = head_rows(j)
            q4_ref[rows] = low[rows, lanes4(j) : lanes4(j) + QUARTER]
            q8_ref[rows] = low[rows, lanes8(j) : lanes8(j) + EIGHTH]

    @pl.when(step >= GROUPS)
    def _():
        low = value.astype(BF)
        qkv_ref[...] = low
        for j in range(GROUP):
            rows = head_rows(j)
            kv4_ref[rows] = low[rows, lanes4(j) : lanes4(j) + QUARTER]
            kvr_ref[rows] = low[rows, rest2(j) : rest2(j) + QUARTER]


def params(limit=24, semantics=None):
    return pltpu.CompilerParams(vmem_limit_bytes=limit * MIB)


def cost(macs, bytes_accessed, exps=0):
    return pl.CostEstimate(
        flops=int(2 * macs), bytes_accessed=int(bytes_accessed), transcendentals=int(exps)
    )


def shaped(rows, width, kind):
    return jax.ShapeDtypeStruct((rows, width), kind)


def whole(height, width):
    return pl.BlockSpec((height, width), lambda i: (0, 0))


def embed(tokens, mask_row, vectors, weight, order):
    query = lambda i: (jnp.minimum(i, GROUPS - 1), 0)
    other = lambda i: (jnp.maximum(i - GROUPS, 0), 0)
    return pl.pallas_call(
        embed_kernel,
        grid=(3 * GROUPS,),
        in_specs=[
            whole(TILES, D), whole(1, TILES), whole(16, D),
            pl.BlockSpec((D, ROWS), lambda i: (0, i)), whole(TILES, TILES),
        ],
        out_specs=[
            whole(D, TILES), whole(TILES, D), whole(8, D),
            pl.BlockSpec((ROWS, TILES), lambda i: (i, 0)),
            pl.BlockSpec((ROWS, QUARTER), query), pl.BlockSpec((ROWS, EIGHTH), query),
            pl.BlockSpec((ROWS, QUARTER), other), pl.BlockSpec((ROWS, QUARTER), other),
        ],
        out_shape=[
            shaped(D, TILES, BF), shaped(TILES, D, BF), shaped(8, D, F32),
            shaped(3 * D, TILES, BF), shaped(D, QUARTER, BF), shaped(D, EIGHTH, BF),
            shaped(2 * D, QUARTER, BF), shaped(2 * D, QUARTER, BF),
        ],
        name="embed",
        compiler_params=params(48),
        cost_estimate=cost(TILES * D * (3 * D + TILES), 20 * MIB),
    )(tokens, mask_row, vectors, weight, order)


def forward0_kernel(q_ref, k_ref, v_ref, kt_ref, qt_ref, o_ref, l_ref):
    keys = stack(k_ref[...], kt_ref[...]).T
    values = stack(v_ref[...], value_rows(TILES))
    block = 512
    for i in range(TILES // block):
        cut = slice(i * block, (i + 1) * block)
        out, total = attend(keys, values, stack(q_ref[:, cut], qt_ref[:, cut]))
        o_ref[:, cut] = out
        l_ref[0, :, cut] = total


def forward1_kernel(qa_ref, qb_ref, k4_ref, v4_ref, kr_ref, vr_ref, kt_ref, qt_ref, o_ref, l_ref):
    for j, q_ref in enumerate((qa_ref, qb_ref)):
        rows = head_rows(j)
        keys = stack(beside(k4_ref[rows], kr_ref[rows]), kt_ref[...]).T
        values = stack(beside(v4_ref[rows], vr_ref[rows]), value_rows(HALF))
        out, total = attend(keys, values, stack(q_ref[...], qt_ref[...]))
        o_ref[rows] = out
        l_ref[j] = total


def forward23_kernel(
    q2_ref, q3a_ref, q3b_ref, k4_ref, v4_ref, k4f_ref, v4f_ref, k8_ref, v8_ref, k8f_ref, v8f_ref,
    kt_ref, qt_ref, z2_ref, z3a_ref, z3b_ref,
):
    table = kt_ref[...]
    zeros = jnp.zeros((16, QUARTER), BF)
    for j in range(4):
        rows, outs = head_rows(j), head_rows(j, AUG)
        keys = beside(stack(k4_ref[rows], table), stack(k4f_ref[rows], table)).T
        values = stack(beside(v4_ref[rows], v4f_ref[rows]), value_rows(HALF))
        out, total = attend(keys, values, stack(q2_ref[rows], qt_ref[...]))
        z2_ref[outs] = stack(out, split_rows(total)).astype(BF)
        keys = stack(beside(k8_ref[rows], k8f_ref[rows]), zeros).T
        values = stack(beside(v8_ref[rows], v8f_ref[rows]), value_rows(QUARTER))
        queries = stack(beside(q3a_ref[rows], q3b_ref[rows]), zeros)
        out, total = attend(keys, values, queries)
        packed = stack(out, split_rows(total)).astype(BF)
        z3a_ref[outs] = packed[:, :EIGHTH]
        z3b_ref[outs] = packed[:, EIGHTH:]


def merge_kernel(
    o0_ref, l0_ref, o1_ref, l1_ref, z2_ref, z3a_ref, z3b_ref, a_ref, r_ref, l_ref
):
    for j in range(GROUP):
        rows, packs = head_rows(j), head_rows(j, AUG)
        start2, start4, start8 = lanes2(j), lanes4(j), lanes8(j)
        other8 = start4 + EIGHTH - (start8 - start4)

        def own(first, count):
            cut = slice(first, first + count)
            return o0_ref[rows, cut], l0_ref[j, :, cut]

        def pair(first, count):
            cut = slice(first - start2, first - start2 + count)
            return o1_ref[rows, cut], l1_ref[j, :, cut]

        def sent(ref, first, count):
            packed = ref[packs, first : first + count].astype(F32)
            return packed[:HD], jnp.sum(packed[HD : HD + 3], axis=0, keepdims=True)

        def write(first, count, parts):
            peak = parts[0][1]
            for _, total in parts[1:]:
                peak = jnp.maximum(peak, total)
            weights = [jnp.exp2(total - peak) for _, total in parts]
            weight_sum = sum(weights[1:], weights[0])
            inverse = 1.0 / weight_sum
            merged = parts[0][0] * (weights[0] * inverse)
            for (out, _), weight in zip(parts[1:], weights[1:]):
                merged = merged + out * (weight * inverse)
            cut = slice(first, first + count)
            low = merged.astype(BF)
            a_ref[rows, cut] = low
            r_ref[rows, cut] = (merged - low.astype(F32)).astype(BF)
            l_ref[j, :, cut] = peak + jnp.log2(weight_sum)

        far = HALF - start2
        cut = slice(far, far + HALF)
        low = o0_ref[rows, cut].astype(BF)
        a_ref[rows, cut] = low
        r_ref[rows, cut] = (o0_ref[rows, cut] - low.astype(F32)).astype(BF)
        l_ref[j, :, cut] = l0_ref[j, :, cut]
        first = rest2(j)
        write(first, QUARTER, [own(first, QUARTER), pair(first, QUARTER)])
        first = other8
        write(first, EIGHTH, [own(first, EIGHTH), pair(first, EIGHTH), sent(z2_ref, first - start4, EIGHTH)])
        first = start8
        write(
            first, EIGHTH,
            [own(first, EIGHTH), pair(first, EIGHTH), sent(z2_ref, first - start4, EIGHTH),
             sent(z3a_ref, 0, EIGHTH), sent(z3b_ref, 0, EIGHTH)],
        )


def rows_of(height, width, lane_block=None, first=0):
    chosen = lane_block or (lambda i: 0)
    return pl.BlockSpec((height, width), lambda i: (i + first, chosen(i)))


def table_spec(width, index):
    return pl.BlockSpec((16, width), lambda i: (index(i), 0))


def totals_spec(heads, width, first=0):
    return pl.BlockSpec((heads, 1, width), lambda i: (i + first, 0, 0))


def totals_shape(heads, width):
    return jax.ShapeDtypeStruct((heads, 1, width), F32)


PAIRS = HEADS * TILES * TILES


def forward_own(qkv, tables, group):
    first = group * GROUP
    return pl.pallas_call(
        forward0_kernel,
        grid=(GROUP,),
        in_specs=[
            rows_of(HD, TILES, None, first), rows_of(HD, TILES, None, HEADS + first),
            rows_of(HD, TILES, None, 2 * HEADS + first),
            table_spec(TILES, lambda i: i & 7), table_spec(TILES, lambda i: i & 7),
        ],
        out_specs=[rows_of(HD, TILES), totals_spec(1, TILES)],
        out_shape=[shaped(ROWS, TILES, F32), totals_shape(GROUP, TILES)],
        name="forward_own",
        compiler_params=params(),
        cost_estimate=cost(PAIRS // 2 * 600, 4 * MIB, PAIRS // 2),
    )(qkv, qkv, qkv, *tables)


def forward_pair(qkv, kv4, kvr, key_table, query_table):
    pair = rows_of(2 * HD, QUARTER)
    pair_v = rows_of(2 * HD, QUARTER, None, HEADS // 2)
    return pl.pallas_call(
        forward1_kernel,
        grid=(HEADS // 2,),
        in_specs=[
            pl.BlockSpec((HD, HALF), lambda i: (2 * i, 0)),
            pl.BlockSpec((HD, HALF), lambda i: (2 * i + 1, 1)),
            pair, pair_v, pair, pair_v,
            table_spec(HALF, lambda i: i & 3), table_spec(HALF, lambda i: i & 3),
        ],
        out_specs=[rows_of(2 * HD, HALF), totals_spec(2, HALF)],
        out_shape=[shaped(D, HALF, F32), totals_shape(HEADS, HALF)],
        name="forward_pair",
        compiler_params=params(),
        cost_estimate=cost(PAIRS // 4 * 600, 5 * MIB, PAIRS // 4),
    )(qkv, qkv, kv4, kv4, kvr, kvr, key_table, query_table)


FOUR = HEADS // 4
NEAR = (
    rows_of(4 * HD, QUARTER), rows_of(4 * HD, QUARTER, None, FOUR),
    rows_of(4 * HD, QUARTER), rows_of(4 * HD, QUARTER, None, FOUR),
    rows_of(4 * HD, EIGHTH, lambda i: i & 1), rows_of(4 * HD, EIGHTH, lambda i: i & 1, FOUR),
    rows_of(4 * HD, EIGHTH, lambda i: i & 1), rows_of(4 * HD, EIGHTH, lambda i: i & 1, FOUR),
)


def near_args(own, far):
    return (own, own, far, far, own, own, far, far)


def forward_sent(q2, q3a, q3b, own, far, tables):
    return pl.pallas_call(
        forward23_kernel,
        grid=(FOUR,),
        in_specs=[
            rows_of(4 * HD, QUARTER), rows_of(4 * HD, EIGHTH), rows_of(4 * HD, EIGHTH), *NEAR,
            table_spec(QUARTER, lambda i: i & 1), table_spec(QUARTER, lambda i: i & 1),
        ],
        out_specs=[rows_of(4 * AUG, QUARTER), rows_of(4 * AUG, EIGHTH), rows_of(4 * AUG, EIGHTH)],
        out_shape=[
            shaped(HEADS * AUG, QUARTER, BF), shaped(HEADS * AUG, EIGHTH, BF),
            shaped(HEADS * AUG, EIGHTH, BF),
        ],
        name="forward_sent",
        compiler_params=params(),
        cost_estimate=cost(PAIRS * 3 // 16 * 600, 4 * MIB, PAIRS * 3 // 16),
    )(q2, q3a, q3b, *near_args(own, far), *tables)


def merge(o0, l0, o1, l1, z2, z3a, z3b, group):
    return pl.pallas_call(
        merge_kernel,
        grid=(1,),
        in_specs=[
            whole(ROWS, TILES), totals_spec(GROUP, TILES),
            rows_of(ROWS, HALF, None, group), totals_spec(GROUP, HALF, group),
            rows_of(GROUP * AUG, QUARTER, None, group), rows_of(GROUP * AUG, EIGHTH, None, group),
            rows_of(GROUP * AUG, EIGHTH, None, group),
        ],
        out_specs=[whole(ROWS, TILES), whole(ROWS, TILES), totals_spec(GROUP, TILES)],
        out_shape=[shaped(ROWS, TILES, BF), shaped(ROWS, TILES, BF), totals_shape(GROUP, TILES)],
        name="merge",
        compiler_params=params(32),
        cost_estimate=cost(TILES * D * 10, 8 * MIB),
    )(o0, l0, o1, l1, z2, z3a, z3b)


ERFCX = (
    0.25388073921203613, 0.254069447517395, 0.22542551159858704, 0.19709868729114532,
    0.02506333962082863, 0.2244575172662735, -0.2487541288137436, 0.06875886023044586,
)


def gelu_pair(x):
    z = jnp.abs(x) * (0.5**0.5)
    t = 1.0 / (1.0 + 0.45 * z)
    series = jnp.full_like(t, 0.5 * ERFCX[-1])
    for factor in reversed(ERFCX[:-1]):
        series = series * t + 0.5 * factor
    bell = jnp.exp(-z * z)
    tail = bell * (t * series)
    below = jnp.where(x < 0.0, tail, 1.0 - tail)
    return x * below, below + x * (bell * 0.3989422804014327)


CHUNK = 768


def feed_kernel(
    order_ref, attn_a_ref, attn_b_ref, start_ref, mask_ref, cot_ref, vec_ref, proj_ref, up_ref, down_ref,
    out_ref, act_ref, pre_ref, normed_ref, attn_ref, mid_ref, sum_ref,
):
    step = pl.program_id(0)
    order = order_ref[...]
    attn = beside(nt(order, attn_a_ref[...]).astype(BF), nt(order, attn_b_ref[...]).astype(BF))
    attn_ref[...] = attn
    visible = column(1.0 - mask_ref[...].astype(F32), D)
    middle = start_ref[...].astype(F32) + nn(attn, proj_ref[...]) + vec_ref[0:1]
    hat, scale = normalise(middle)
    gain = vec_ref[4:5]
    normed = (hat * gain + vec_ref[5:6]).astype(BF)
    normed_ref[...] = normed
    cot = cot_ref[...]
    final = middle + vec_ref[1:2]
    back = jnp.zeros_like(middle)
    sums = []
    for c in range(up_ref.shape[1] // CHUNK):
        cut = slice(c * CHUNK, (c + 1) * CHUNK)
        pre = nn(normed, up_ref[:, cut]) + vec_ref[8 + c : 9 + c]
        act, slope = gelu_pair(pre)
        act = act.astype(BF)
        act_ref[:, cut] = act
        grad = (slope * nt(cot, down_ref[cut, :])).astype(BF)
        pre_ref[:, cut] = grad
        sums.append(jnp.sum(grad.astype(F32), axis=0, keepdims=True))
        final = final + nn(act, down_ref[cut, :])
        back = back + nt(grad, up_ref[:, cut])
    out_ref[...] = final.astype(BF)
    cot = cot.astype(F32)
    hat_grad = back * gain
    first = jnp.mean(hat_grad, axis=1, keepdims=True)
    second = jnp.mean(hat_grad * hat, axis=1, keepdims=True)
    mid_grad = cot + scale * (hat_grad - first - hat * second)
    mid_ref[...] = mid_grad
    for value in (
        mid_grad.astype(BF).astype(F32), cot, back * hat, back,
        visible * middle * middle, visible * final * final,
    ):
        sums.append(jnp.sum(value, axis=0, keepdims=True))
    sums.append(jnp.zeros((16 - len(sums), D), F32))
    sums = stack(*sums)

    @pl.when(step == 0)
    def _():
        sum_ref[...] = sums

    @pl.when(step > 0)
    def _():
        sum_ref[...] += sums


def once(height, width):
    return pl.BlockSpec((height, width), lambda i: (0, 0), pipeline_mode=pl.Buffered(1))


def feed(order, attn_a, attn_b, start, mask_row, cot, vectors, proj, up, down):
    ff = up.shape[1]
    block = 256
    part = lambda width: pl.BlockSpec((block, width), lambda i: (i, 0))
    return pl.pallas_call(
        feed_kernel,
        grid=(TILES // block,),
        in_specs=[
            part(TILES), once(ROWS, TILES), once(ROWS, TILES), part(D),
            pl.BlockSpec((1, block), lambda i: (0, i)), part(D), once(16, D), once(D, D),
            once(D, ff), once(ff, D),
        ],
        out_specs=[part(D), part(ff), part(ff), part(D), part(D), part(D), whole(16, D)],
        out_shape=[
            shaped(TILES, D, BF), shaped(TILES, ff, BF), shaped(TILES, ff, BF), shaped(TILES, D, BF),
            shaped(TILES, D, BF), shaped(TILES, D, F32), shaped(16, D, F32),
        ],
        name="feed",
        compiler_params=params(56),
        cost_estimate=cost(TILES * D * (4 * ff + D + TILES), 36 * MIB, TILES * ff),
    )(order, attn_a, attn_b, start, mask_row, cot, vectors, proj, up, down)


def branch_kernel(
    mid_ref, proj_ref, order_ref, a_ref, r_ref, l_ref, g_ref, g4_ref, g8_ref
):
    grad = nt(proj_ref[...], mid_ref[...].astype(BF)).astype(BF)
    grad = nn(grad, order_ref[...])
    for j in range(GROUP):
        rows, packs = head_rows(j), head_rows(j, AUG)
        merged = a_ref[rows].astype(F32) + r_ref[rows].astype(F32)
        inner = jnp.sum(grad[rows] * merged, axis=0, keepdims=True)
        packed = stack(grad[rows], split_rows(-inner, -l_ref[j])).astype(BF)
        g_ref[packs] = packed
        g4_ref[packs] = packed[:, lanes4(j) : lanes4(j) + QUARTER]
        g8_ref[packs] = packed[:, lanes8(j) : lanes8(j) + EIGHTH]


def branch(mid, proj, order, attn, rest, total, group):
    return pl.pallas_call(
        branch_kernel,
        grid=(1,),
        in_specs=[
            whole(TILES, D), rows_of(ROWS, D, None, group), whole(TILES, TILES),
            whole(ROWS, TILES), whole(ROWS, TILES), totals_spec(GROUP, TILES),
        ],
        out_specs=[whole(GROUP * AUG, TILES), whole(GROUP * AUG, QUARTER), whole(GROUP * AUG, EIGHTH)],
        out_shape=[
            shaped(GROUP * AUG, TILES, BF), shaped(GROUP * AUG, QUARTER, BF),
            shaped(GROUP * AUG, EIGHTH, BF),
        ],
        name="branch",
        compiler_params=params(40),
        cost_estimate=cost(TILES * ROWS * (D + TILES), 9 * MIB),
    )(mid, proj, order, attn, rest, total)


def weights_kernel(
    act_ref, cot_ref, normed_ref, pre_ref, attn_ref, mid_ref, out_ref, turned_n, turned_a, low, spare
):
    @pl.when(pl.program_id(0) == 0)
    def _():
        turned_n[...] = normed_ref[...].T
        turned_a[...] = attn_ref[...].T
        low[...] = mid_ref[...].astype(BF)

    block = out_ref.shape[0]
    rows = pl.ds(pl.multiple_of(pl.program_id(0) * block, block), block)
    ff = pre_ref.shape[1]
    out_ref[:, :ff] = nn(turned_n[rows], pre_ref[...]).astype(BF)
    out_ref[:, ff : ff + D] = nn(turned_a[rows], low[...]).astype(BF)
    folds = ff // D
    down = tn(act_ref[...], cot_ref[...])
    for k in range(D // 128):
        spare[k] = down[:, k * 128 : (k + 1) * 128]
    for j in range(folds):
        for k in range(D // 128):
            first = ff + D + j * D + k * 128
            piece = spare[k, pl.ds(j, block, stride=folds), :]
            out_ref[:, first : first + 128] = piece.astype(BF)


def weight_grads(act, cot, normed, pre, attn, mid):
    ff = act.shape[1]
    block = 128
    width = 2 * ff + D
    return pl.pallas_call(
        weights_kernel,
        grid=(D // block,),
        in_specs=[
            pl.BlockSpec((TILES, block * (ff // D)), lambda i: (0, i)), once(TILES, D), once(TILES, D),
            once(TILES, ff), once(TILES, D), once(TILES, D),
        ],
        out_specs=pl.BlockSpec((block, width), lambda i: (i, 0)),
        out_shape=shaped(D, width, BF),
        scratch_shapes=[
            pltpu.VMEM((D, TILES), BF), pltpu.VMEM((D, TILES), BF), pltpu.VMEM((TILES, D), BF),
            pltpu.VMEM((D // 128, block * (ff // D), 128), F32),
        ],
        name="weight_grads",
        compiler_params=params(48),
        cost_estimate=cost(TILES * D * (2 * ff + D), 32 * MIB),
    )(act, cot, normed, pre, attn, mid)


def back_block(keys, values, keys_t, queries, queries_plain, grads):
    probs = jnp.exp2(nn(keys, queries))
    grad_scores = (probs * nn(values, grads)).astype(BF)
    probs = probs.astype(BF)
    grad_q = nn(keys_t, grad_scores) * SCALE
    grad_k = nt(queries_plain, grad_scores) * LN2
    grad_v = nt(grads[:HD], probs)
    return grad_q, grad_k, grad_v


def back1_kernel(
    qa_ref, qb_ref, ga_ref, gb_ref, k4_ref, v4_ref, kr_ref, vr_ref, kt_ref, qt_ref,
    dq_ref, dk_ref, dv_ref,
):
    for j, (q_ref, g_ref) in enumerate(((qa_ref, ga_ref), (qb_ref, gb_ref))):
        rows = head_rows(j)
        keys_t = beside(k4_ref[rows], kr_ref[rows])
        keys = stack(keys_t, kt_ref[...]).T
        values = stack(beside(v4_ref[rows], vr_ref[rows]), value_rows(HALF)).T
        grads = g_ref[...]
        queries = stack(q_ref[...], grads[HD:] + qt_ref[...])
        dq_ref[rows], dk_ref[rows], dv_ref[rows] = back_block(
            keys, values, keys_t, queries, q_ref[...], grads
        )


def back23_kernel(
    q2_ref, q3a_ref, q3b_ref, g2_ref, g3a_ref, g3b_ref,
    k4_ref, v4_ref, k4f_ref, v4f_ref, k8_ref, v8_ref, k8f_ref, v8f_ref, kt_ref, qt_ref,
    dk1_ref, dv1_ref,
    dq2_ref, dq3a_ref, dq3b_ref, dk_ref, dv_ref, fara_ref, farb_ref,
):
    step = pl.program_id(0)
    table = kt_ref[...]
    row = lax.broadcasted_iota(jnp.int32, (16, QUARTER), 0)
    plain = jnp.where((row >= 3) & (row < 6), 1.0, 0.0).astype(BF)
    lane = lax.broadcasted_iota(jnp.int32, (1, QUARTER), 1)
    inside = (lane >= EIGHTH) == ((step & 1) == 1)
    for j in range(4):
        rows, packs = head_rows(j), head_rows(j, AUG)
        keys_t = beside(k4_ref[rows], k4f_ref[rows])
        keys = stack(keys_t, beside(table, table)).T
        values = stack(beside(v4_ref[rows], v4f_ref[rows]), value_rows(HALF)).T
        grads = g2_ref[packs]
        queries = stack(q2_ref[rows], grads[HD:] + qt_ref[...])
        dq, dk4, dv4 = back_block(keys, values, keys_t, queries, q2_ref[rows], grads)
        dq2_ref[rows] = dq.astype(BF)
        keys_t = beside(k8_ref[rows], k8f_ref[rows])
        keys = stack(keys_t, plain).T
        values = stack(beside(v8_ref[rows], v8f_ref[rows]), value_rows(QUARTER)).T
        grads = beside(g3a_ref[packs], g3b_ref[packs])
        plain_q = beside(q3a_ref[rows], q3b_ref[rows])
        queries = stack(plain_q, grads[HD:])
        dq, dk8, dv8 = back_block(keys, values, keys_t, queries, plain_q, grads)
        dq3a_ref[rows] = dq[:, :EIGHTH].astype(BF)
        dq3b_ref[rows] = dq[:, EIGHTH:].astype(BF)
        for kind, own_ref, one_ref, four, eight in (
            (0, dk_ref, dk1_ref, dk4, dk8),
            (1, dv_ref, dv1_ref, dv4, dv8),
        ):
            near, away = eight[:, :EIGHTH], eight[:, EIGHTH:]
            own_ref[rows] = four[:, :QUARTER] + jnp.where(inside, beside(near, near), 0.0)
            extra = four[:, QUARTER:] + jnp.where(inside, beside(away, away), 0.0)
            far = beside(one_ref[rows, :QUARTER] + extra, one_ref[rows, QUARTER:]).astype(BF)

            @pl.when(step < FOUR // GROUPS)
            def _(kind=kind, rows=rows, far=far):
                fara_ref[kind, rows] = far

            @pl.when(step >= FOUR // GROUPS)
            def _(kind=kind, rows=rows, far=far):
                farb_ref[kind, rows] = far


def back0_kernel(q_ref, g_ref, k_ref, v_ref, kt_ref, qt_ref, dq_ref, dk_ref, dv_ref):
    keys_t = k_ref[...]
    keys = stack(keys_t, kt_ref[...]).T
    values = stack(v_ref[...], value_rows(TILES)).T
    block = 512
    dk = dv = None
    for i in range(TILES // block):
        cut = slice(i * block, (i + 1) * block)
        grads = g_ref[:, cut]
        plain_q = q_ref[:, cut]
        queries = stack(plain_q, grads[HD:] + qt_ref[:, cut])
        dq, more_k, more_v = back_block(keys, values, keys_t, queries, plain_q, grads)
        dq_ref[:, cut] = dq.astype(BF)
        dk = more_k if dk is None else dk + more_k
        dv = more_v if dv is None else dv + more_v
    dk_ref[...] = dk.astype(BF)
    dv_ref[...] = dv.astype(BF)


def back_pair(qkv, grads, kv4, kvr, key_table, query_table):
    pair = rows_of(2 * HD, QUARTER)
    pair_v = rows_of(2 * HD, QUARTER, None, HEADS // 2)
    out = rows_of(2 * HD, HALF)
    even = lambda height: pl.BlockSpec((height, HALF), lambda i: (2 * i, 0))
    odd = lambda height: pl.BlockSpec((height, HALF), lambda i: (2 * i + 1, 1))
    return pl.pallas_call(
        back1_kernel,
        grid=(HEADS // 2,),
        in_specs=[
            even(HD), odd(HD), even(AUG), odd(AUG), pair, pair_v, pair, pair_v,
            table_spec(HALF, lambda i: i & 3), table_spec(HALF, lambda i: i & 3),
        ],
        out_specs=[out] * 3,
        out_shape=[shaped(D, HALF, F32)] * 3,
        name="back_pair",
        compiler_params=params(),
        cost_estimate=cost(PAIRS // 4 * 900, 12 * MIB, PAIRS // 4),
    )(qkv, qkv, grads, grads, kv4, kv4, kvr, kvr, key_table, query_table)


def back_sent(q2, q3a, q3b, g2, g3a, g3b, own, far, tables, dk1, dv1):
    quarter, eighth, half = (rows_of(4 * HD, w) for w in (QUARTER, EIGHTH, HALF))
    steps = FOUR // GROUPS
    return pl.pallas_call(
        back23_kernel,
        grid=(FOUR,),
        in_specs=[
            quarter, eighth, eighth,
            rows_of(4 * AUG, QUARTER), rows_of(4 * AUG, EIGHTH), rows_of(4 * AUG, EIGHTH), *NEAR,
            table_spec(QUARTER, lambda i: i & 1), table_spec(QUARTER, lambda i: i & 1), half, half,
        ],
        out_specs=[
            quarter, eighth, eighth, quarter, quarter,
            pl.BlockSpec((2, 4 * HD, HALF), lambda i: (0, jnp.minimum(i, steps - 1), 0)),
            pl.BlockSpec((2, 4 * HD, HALF), lambda i: (0, jnp.maximum(i - steps, 0), 0)),
        ],
        out_shape=[
            shaped(D, QUARTER, BF), shaped(D, EIGHTH, BF), shaped(D, EIGHTH, BF),
            shaped(D, QUARTER, F32), shaped(D, QUARTER, F32),
            jax.ShapeDtypeStruct((2, ROWS, HALF), BF), jax.ShapeDtypeStruct((2, ROWS, HALF), BF),
        ],
        name="back_sent",
        compiler_params=params(32),
        cost_estimate=cost(PAIRS * 3 // 16 * 900, 12 * MIB, PAIRS * 3 // 16),
    )(q2, q3a, q3b, g2, g3a, g3b, *near_args(own, far), *tables, dk1, dv1)


def back_own(qkv, grads, tables, group):
    first = group * GROUP
    full = rows_of(HD, TILES)
    return pl.pallas_call(
        back0_kernel,
        grid=(GROUP,),
        in_specs=[
            rows_of(HD, TILES, None, first), rows_of(AUG, TILES),
            rows_of(HD, TILES, None, HEADS + first), rows_of(HD, TILES, None, 2 * HEADS + first),
            table_spec(TILES, lambda i: i & 7), table_spec(TILES, lambda i: i & 7),
        ],
        out_specs=[full, full, full],
        out_shape=[shaped(ROWS, TILES, BF)] * 3,
        name="back_own",
        compiler_params=params(),
        cost_estimate=cost(PAIRS // 2 * 900, 7 * MIB, PAIRS // 2),
    )(qkv, grads, qkv, qkv, *tables)


def collect_kernel(
    dq_ref, dk_ref, dv_ref, dq1_ref, dq2_ref, dq3a_ref, dq3b_ref, dk4_ref, dv4_ref, far_ref,
    normed_ref, w_ref, grad_ref, back_ref, value_ref,
):
    step = pl.program_id(0)

    def write(base_ref, parts):
        for j in range(GROUP):
            rows = head_rows(j)
            pieces = {first: base_ref[rows, first : first + EIGHTH].astype(F32) for first in range(0, TILES, EIGHTH)}
            for ref, first, source, count in parts(j):
                for k in range(0, count, EIGHTH):
                    pieces[first + k] = pieces[first + k] + ref[rows, source + k : source + k + EIGHTH].astype(F32)
            value_ref[rows] = beside(*(pieces[first] for first in range(0, TILES, EIGHTH))).astype(BF)

    @pl.when(step == 0)
    def _():
        write(
            dq_ref,
            lambda j: (
                (dq1_ref, lanes2(j), 0, HALF), (dq2_ref, lanes4(j), 0, QUARTER),
                (dq3a_ref, lanes8(j), 0, EIGHTH), (dq3b_ref, lanes8(j), 0, EIGHTH),
            ),
        )

    for at, base_ref, own_ref, far_ref in ((1, dk_ref, dk4_ref, far_ref.at[0]), (2, dv_ref, dv4_ref, far_ref.at[1])):

        @pl.when(step == at)
        def _(base_ref=base_ref, own_ref=own_ref, far_ref=far_ref):
            write(
                base_ref,
                lambda j: (
                    (own_ref, lanes4(j), 0, QUARTER), (far_ref, lanes4(j), 0, QUARTER),
                    (far_ref, rest2(j), QUARTER, QUARTER),
                ),
            )

    value = value_ref[...]
    grad_ref[...] = nt(normed_ref[...], value).astype(BF)
    back = nn(w_ref[...], value)

    @pl.when(step == 0)
    def _():
        back_ref[...] = back

    @pl.when(step > 0)
    def _():
        back_ref[...] += back


def collect(dq, dk, dv, dq1, dq2, dq3a, dq3b, dk4, dv4, far, normed, weight, group):
    return pl.pallas_call(
        collect_kernel,
        grid=(3,),
        in_specs=[
            whole(ROWS, TILES), whole(ROWS, TILES), whole(ROWS, TILES),
            pl.BlockSpec((ROWS, HALF), lambda i: (group, 0)),
            pl.BlockSpec((ROWS, QUARTER), lambda i: (group, 0)),
            pl.BlockSpec((ROWS, EIGHTH), lambda i: (group, 0)),
            pl.BlockSpec((ROWS, EIGHTH), lambda i: (group, 0)),
            pl.BlockSpec((ROWS, QUARTER), lambda i: (group, 0)),
            pl.BlockSpec((ROWS, QUARTER), lambda i: (group, 0)),
            pl.BlockSpec((2, ROWS, HALF), lambda i: (0, 0, 0)),
            whole(D, TILES), pl.BlockSpec((D, ROWS), lambda i: (0, 2 * i + group)),
        ],
        out_specs=[pl.BlockSpec((D, ROWS), lambda i: (0, i)), whole(D, TILES)],
        out_shape=[shaped(D, 3 * ROWS, BF), shaped(D, TILES, F32)],
        scratch_shapes=[pltpu.VMEM((ROWS, TILES), BF)],
        name="collect",
        compiler_params=params(40),
        cost_estimate=cost(3 * ROWS * TILES * D * 2, 16 * MIB),
    )(dq, dk, dv, dq1, dq2, dq3a, dq3b, dk4, dv4, far, normed, weight)


def finish_kernel(back_a_ref, back_b_ref, order_ref, start_ref, mask_ref, mid_ref, vec_ref, out_ref, sum_ref):
    step = pl.program_id(0)
    turned = (back_a_ref[...] + back_b_ref[...]).astype(BF)
    back = nt(order_ref[...], turned)
    hidden = column(mask_ref[...].astype(F32), D) > 0.5
    hat, scale = normalise(start_ref[...].astype(F32))
    hat_grad = back * vec_ref[2:3]
    first = jnp.mean(hat_grad, axis=1, keepdims=True)
    second = jnp.mean(hat_grad * hat, axis=1, keepdims=True)
    grad = mid_ref[...] + scale * (hat_grad - first - hat * second)
    out_ref[...] = jnp.where(hidden, 0.0, grad).astype(BF)
    sums = stack(
        jnp.sum(back * hat, axis=0, keepdims=True),
        jnp.sum(back, axis=0, keepdims=True),
        jnp.sum(jnp.where(hidden, grad, 0.0), axis=0, keepdims=True),
        jnp.zeros((5, D), F32),
    )

    @pl.when(step == 0)
    def _():
        sum_ref[...] = sums

    @pl.when(step > 0)
    def _():
        sum_ref[...] += sums


def finish(back_a, back_b, order, start, mask_row, mid, vectors):
    block = 256
    part = lambda width: pl.BlockSpec((block, width), lambda i: (i, 0))
    return pl.pallas_call(
        finish_kernel,
        grid=(TILES // block,),
        in_specs=[
            whole(D, TILES), whole(D, TILES), part(TILES), part(D),
            pl.BlockSpec((1, block), lambda i: (0, i)), part(D), whole(16, D),
        ],
        out_specs=[part(D), whole(8, D)],
        out_shape=[shaped(TILES, D, BF), shaped(8, D, F32)],
        name="finish",
        compiler_params=params(40),
        cost_estimate=cost(TILES * TILES * D, 16 * MIB),
    )(back_a, back_b, order, start, mask_row, mid, vectors)


def exchange(value, axis, mask):
    pairs = [(source, source ^ mask) for source in range(lax.axis_size(axis))]
    return lax.ppermute(value, axis, pairs)


def after(value, *others):
    return lax.optimization_barrier((value,) + others)[0]


def after_all(values, *others):
    return lax.optimization_barrier(tuple(values) + others)[: len(values)]


def halve(value, dim, axis, bit):
    mine = lax.axis_index(axis) >> bit & 1
    half = value.shape[dim] // 2
    send = lax.dynamic_slice_in_dim(value, (1 - mine) * half, half, dim)
    keep = lax.dynamic_slice_in_dim(value, mine * half, half, dim)
    got = exchange(send, axis, 1 << bit)
    return (keep.astype(F32) + got.astype(F32)).astype(BF)


def join(value, dim, axis, bit):
    mine = lax.axis_index(axis) >> bit & 1
    got = exchange(value, axis, 1 << bit)
    first = jnp.where(mine == 0, value, got)
    second = jnp.where(mine == 0, got, value)
    return jnp.concatenate([first, second], axis=dim)


def log2_size(axis):
    return (lax.axis_size(axis) - 1).bit_length()


def reduce_blocks(blocks):
    value = blocks
    for bit in range(log2_size("dp")):
        value = halve(value, 1, "dp", bit)
    for bit in reversed(range(log2_size("seq"))):
        value = halve(value, 0, "seq", bit)
    value = value[0]
    for bit in reversed(range(log2_size("dp"))):
        value = join(value, 0, "dp", bit)
    return value.astype(F32)


def in_blocks(grad):
    count = lax.axis_size("seq")
    return grad.reshape(count, grad.shape[0] // count, -1)


def local(
    tokens, tile_mask, cotangent, qkv_weight, proj_weight, proj_bias, up_weight, up_bias,
    down_weight, down_bias, attn_gain, attn_shift, mlp_gain, mlp_shift, mask_vector,
):
    order = order_matrix()
    tables0 = weight_tables(0)
    query_table1 = weight_tables(1)[1]
    key_table1 = weight_tables(1, True)[0]
    tables2 = weight_tables(2)
    row = jnp.zeros((D,), BF)
    vectors = jnp.concatenate(
        [proj_bias, down_bias, attn_gain, attn_shift, mlp_gain, mlp_shift, mask_vector, row, up_bias,
         jnp.zeros((16 * D - 8 * D - up_bias.shape[0],), BF)]
    ).astype(F32).reshape(16, D)
    seq_count = lax.axis_size("seq")

    normed_t, start, token_squares, qkv, q4, q8, kv4, kvr = embed(
        tokens[0], tile_mask, vectors, qkv_weight, order
    )
    q2 = exchange(q4, "seq", 2)
    q3a = exchange(q8, "seq", 4)
    q3b = exchange(q8, "seq", 6)
    kv4_far = exchange(kv4, "seq", 1)
    kvr_far = exchange(after(kvr, kv4_far), "seq", 1)
    out0a, total0a = forward_own(qkv, tables0, 0)
    z2, z3a, z3b = forward_sent(q2, q3a, q3b, kv4, kv4_far, after_all(tables2, total0a))
    later = after_all(tables0, z2)
    z2 = exchange(z2, "seq", 2)
    z3a = exchange(z3a, "seq", 4)
    z3b = exchange(z3b, "seq", 6)
    out0b, total0b = forward_own(qkv, later, 1)
    out1, total1 = forward_pair(qkv, kv4_far, kvr_far, after(key_table1, total0b), query_table1)
    total0a, total0b = after_all((total0a, total0b), total1)
    attn_a, rest_a, total_a = merge(out0a, total0a, out1, total1, z2, z3a, z3b, 0)
    attn_b, rest_b, total_b = merge(out0b, total0b, out1, total1, z2, z3a, z3b, 1)

    layer_out, act, grad_pre, normed2, attn, grad_mid, feed_sums = feed(
        order, attn_a, attn_b, start, tile_mask, cotangent[0], vectors, proj_weight, up_weight, down_weight
    )
    grads_a, g4a, g8a = branch(grad_mid, proj_weight, order, attn_a, rest_a, total_a, 0)
    grads_b, g4b, g8b = branch(grad_mid, proj_weight, order, attn_b, rest_b, total_b, 1)
    g4, g8 = jnp.concatenate([g4a, g4b]), jnp.concatenate([g8a, g8b])
    grads = jnp.concatenate([grads_a, grads_b])
    g2 = exchange(g4, "seq", 2)
    g3a = exchange(g8, "seq", 4)
    g3b = exchange(g8, "seq", 6)
    early = weight_grads(act, cotangent[0], normed2, grad_pre, attn, after(grad_mid, g8))
    later = after(key_table1, early)
    early = lax.psum_scatter(early, ("seq", "dp"), scatter_dimension=0, tiled=True)
    dq1, dk1, dv1 = back_pair(qkv, grads, kv4_far, kvr_far, later, query_table1)
    dq2, dq3a, dq3b, dk4, dv4, far_a, far_b = back_sent(
        q2, q3a, q3b, g2, g3a, g3b, kv4, kv4_far, after_all(tables2, dq1), dk1, dv1
    )
    later = after_all(tables0, far_a)
    far_a = exchange(far_a, "seq", 1)
    far_b = exchange(far_b, "seq", 1)
    dq2 = exchange(dq2, "seq", 2)
    dq3a = exchange(dq3a, "seq", 4)
    dq3b = exchange(dq3b, "seq", 6)
    shared = (dq1, dq2, dq3a, dq3b, dk4, dv4)
    own_a = back_own(qkv, grads_a, later, 0)
    qkv_grad_a, back_a = collect(*own_a, *shared, far_a, normed_t, qkv_weight, 0)
    own_b = back_own(qkv, grads_b, after_all(tables0, qkv_grad_a), 1)
    qkv_grad_b, back_b = collect(*own_b, *shared, far_b, normed_t, qkv_weight, 1)
    early = after(early, qkv_grad_b)
    early = lax.all_gather(early, "dp", axis=0, tiled=True)
    tokens_grad, finish_sums = finish(back_a, back_b, order, start, tile_mask, grad_mid, vectors)

    share = D // seq_count
    ff = up_weight.shape[1]
    pieces = [finish_sums[:3].reshape(3, seq_count, share), feed_sums[4:8].reshape(4, seq_count, share)]
    small = jnp.transpose(jnp.concatenate(pieces), (1, 0, 2)).reshape(seq_count, 7 * share)
    everywhere = jnp.concatenate(
        [token_squares[0], feed_sums[8], feed_sums[9], 1.0 - tile_mask[0].astype(F32)]
    )
    small = jnp.concatenate(
        [small, feed_sums[: ff // D].reshape(seq_count, ff // seq_count),
         jnp.broadcast_to(everywhere[None], (seq_count, everywhere.shape[0]))],
        axis=1,
    )
    width = 3 * ROWS
    rows = 4 * -(-small.shape[1] // (4 * width))
    small = jnp.pad(small, ((0, 0), (0, rows * width - small.shape[1])))
    blocks = jnp.concatenate([in_blocks(qkv_grad_b), small.reshape(seq_count, rows, width).astype(BF)], axis=1)
    summed_a = reduce_blocks(in_blocks(qkv_grad_a))
    summed_b = reduce_blocks(blocks)
    qkv_grad = jnp.stack(
        [summed_a.reshape(share, 3, ROWS), summed_b[:share].reshape(share, 3, ROWS)], axis=2
    ).reshape(share, 3 * D)
    flat = summed_b[share:].reshape(-1)
    gain_grad, shift_grad, mask_grad, proj_bias_grad, down_bias_grad, gain2_grad, shift2_grad = (
        flat[i * share : (i + 1) * share] for i in range(7)
    )
    first = 7 * share
    up_bias_grad = flat[first : first + ff // seq_count]
    first = first + ff // seq_count
    squares = jnp.sum(flat[first : first + 3 * D].reshape(3, D), axis=1)
    count = jnp.sum(flat[first + 3 * D : first + 3 * D + TILES])
    stream_rms = jnp.sqrt(squares / (count * D))
    early = early.astype(F32)
    up_grad, proj_grad = early[:, :ff], early[:, ff : ff + D]
    down_grad = early[:, ff + D :].reshape(-1, D)
    return (
        layer_out[None], tokens_grad[None], qkv_grad, proj_grad, proj_bias_grad, up_grad, up_bias_grad,
        down_grad, down_bias_grad, gain_grad, shift_grad, gain2_grad, shift2_grad, mask_grad, stream_rms,
    )


def solution(mesh):
    rows = P("dp", "seq", None)
    in_specs = (rows, P("dp", "seq"), rows) + (P(),) * 12
    matrix, vector = P("seq", None), P("seq")
    out_specs = (
        rows, rows, matrix, matrix, vector, matrix, vector, matrix,
        vector, vector, vector, vector, vector, vector, P(),
    )
    return jax.shard_map(local, mesh=mesh, in_specs=in_specs, out_specs=out_specs, check_vma=False)
```

```python
import functools

import numpy as np
import jax
import jax.numpy as jnp
from jax import lax
from jax.experimental import pallas as pl
from jax.experimental.pallas import tpu as pltpu
from jax.sharding import PartitionSpec as P

HEADS = 16
HD = 48
AUG = 64
TILES = 1024
EPS = 1e-06
FILL = -1e30
LN2 = float(np.log(2.0))
SCALE = HD**-0.5
QSCALE = SCALE / LN2
BF = jnp.bfloat16
F32 = jnp.float32


def nn(a, b):
    return lax.dot_general(a, b, (((1,), (0,)), ((), ())), preferred_element_type=F32)


def nt(a, b):
    return lax.dot_general(a, b, (((1,), (1,)), ((), ())), preferred_element_type=F32)


def tn(a, b):
    return lax.dot_general(a, b, (((0,), (0,)), ((), ())), preferred_element_type=F32)


GROUP = 8
GROUPS = HEADS // GROUP
D = HEADS * HD
ROWS = GROUP * HD
HALF, QUARTER, EIGHTH = TILES // 2, TILES // 4, TILES // 8
MIB = 1024 * 1024


def place_of(tile):
    return (tile & 1) * HALF + (tile >> 1 & 1) * QUARTER + (tile >> 2 & 1) * EIGHTH + (tile >> 3)


def order_matrix():
    tile = np.arange(TILES)
    matrix = np.zeros((TILES, TILES), np.float32)
    matrix[tile, place_of(tile)] = 1.0
    return jnp.asarray(matrix.astype(jnp.bfloat16))


def lanes2(h):
    return (h & 1) * HALF


def lanes4(h):
    return lanes2(h) + (h >> 1 & 1) * QUARTER


def rest2(h):
    return lanes2(h) + (1 - (h >> 1 & 1)) * QUARTER


def lanes8(h):
    return lanes4(h) + (h >> 2 & 1) * EIGHTH


def weight_tables(level, compact=False):
    count = TILES >> level
    classes = 8 >> level
    totals = {0: [2.0, 3.0, 4.0], 1: [2.0, 3.0], 2: [2.0]}[level]
    lane = np.arange(count)
    key_rows = np.zeros((classes, 16, count), np.float32)
    query_rows = np.zeros((classes, 16, count), np.float32)
    key_rows[:, 3:6] = 1.0
    for c in range(classes):
        inside = np.ones(count, bool)
        before = 1.0
        for i, total in enumerate(totals):
            bit = (lane >> (9 - level - i)) & 1
            wanted = 0 if compact and i == 0 else c >> i & 1
            inside = inside & (bit == wanted)
            step = np.log2(total) - np.log2(before)
            before = total
            high = np.float32(np.asarray(step, np.float32).astype(jnp.bfloat16))
            key_rows[c, 6 + 2 * i] = inside
            key_rows[c, 7 + 2 * i] = inside
            query_rows[c, 6 + 2 * i] = inside * high
            query_rows[c, 7 + 2 * i] = inside * (step - high)
    shape = (classes * 16, count)
    return (
        jnp.asarray(key_rows.reshape(shape).astype(jnp.bfloat16)),
        jnp.asarray(query_rows.reshape(shape).astype(jnp.bfloat16)),
    )


def value_rows(count):
    row = lax.broadcasted_iota(jnp.int32, (16, count), 0)
    return jnp.where(row < 3, 1.0, 0.0).astype(BF)


def stack(*parts):
    return jnp.concatenate(parts, axis=0)


def beside(*parts):
    return jnp.concatenate(parts, axis=1)


def head_rows(j, height=HD):
    return slice(j * height, (j + 1) * height)


SAFE = 60.0


def attend(keys, values, queries, safe):
    scores = nn(keys, queries)
    if safe:
        probs = jnp.exp2(scores).astype(BF)
    else:
        peak = jnp.max(scores, axis=0, keepdims=True)
        probs = jnp.exp2(scores - peak).astype(BF)
    out = nn(values, probs)
    total = out[HD : HD + 1]
    level = jnp.log2(total)
    return out[:HD] / total, level if safe else peak + level


def largest(*refs):
    count = refs[0].shape[0] // HD
    squares = [jnp.square(ref[...].astype(F32)) for ref in refs]
    result = []
    for j in range(count):
        rows = [jnp.sum(square[head_rows(j)], axis=0, keepdims=True) for square in squares]
        top = jnp.max(rows[0])
        for row in rows[1:]:
            top = jnp.maximum(top, jnp.max(row))
        result.append(top)
    return result


def either_way(query_tops, key_tops, body):
    bound = query_tops[0] * key_tops[0]
    for query_top, key_top in zip(query_tops[1:], key_tops[1:]):
        bound = jnp.maximum(bound, query_top * key_top)
    safe = bound < SAFE * SAFE

    @pl.when(safe)
    def _():
        body(True)

    @pl.when(jnp.logical_not(safe))
    def _():
        body(False)


def split3(value):
    high = value.astype(BF).astype(F32)
    rest = value - high
    mid = rest.astype(BF).astype(F32)
    return high, mid, rest - mid


def split_rows(*values):
    row = lax.broadcasted_iota(jnp.int32, (16, values[0].shape[1]), 0)
    packed = jnp.zeros((16, values[0].shape[1]), F32)
    for i, value in enumerate(values):
        for k, piece in enumerate(split3(value)):
            packed = jnp.where(row == 3 * i + k, piece, packed)
    return packed


def column(row, width):
    turned = jnp.broadcast_to(row, (128, row.shape[1])).T
    return jnp.concatenate([turned] * (width // 128), axis=1)


def normalise(value):
    average = jnp.mean(value, axis=1, keepdims=True)
    centred = value - average
    spread = jnp.mean(centred * centred, axis=1, keepdims=True)
    scale = lax.rsqrt(spread + EPS)
    return centred * scale, scale


def embed_kernel(
    tok_ref, mask_ref, fill_ref, gain_ref, shift_ref, w_ref, order_ref,
    normed_ref, start_ref, square_ref, qkv_ref, q4_ref, q8_ref, kv4_ref, kvr_ref,
):
    step = pl.program_id(0)

    @pl.when(step == 0)
    def _():
        hidden = column(mask_ref[...].astype(F32), D) > 0.5
        rows = tok_ref[...].astype(F32)
        start = jnp.where(hidden, as_row(fill_ref), rows)
        start_ref[...] = start.astype(BF)
        squares = jnp.where(hidden, 0.0, rows * rows)
        square_ref[...] = jnp.broadcast_to(jnp.sum(squares, axis=0, keepdims=True), (8, D))
        normed = normalise(start)[0] * as_row(gain_ref) + as_row(shift_ref)
        normed_ref[...] = tn(normed.astype(BF), order_ref[...]).astype(BF)

    value = tn(w_ref[...], normed_ref[...])

    @pl.when(step < GROUPS)
    def _():
        low = (value * QSCALE).astype(BF)
        qkv_ref[...] = low
        for j in range(GROUP):
            rows = head_rows(j)
            q4_ref[rows] = low[rows, lanes4(j) : lanes4(j) + QUARTER]
            q8_ref[rows] = low[rows, lanes8(j) : lanes8(j) + EIGHTH]

    @pl.when(step >= GROUPS)
    def _():
        low = value.astype(BF)
        qkv_ref[...] = low
        for j in range(GROUP):
            rows = head_rows(j)
            kv4_ref[rows] = low[rows, lanes4(j) : lanes4(j) + QUARTER]
            kvr_ref[rows] = low[rows, rest2(j) : rest2(j) + QUARTER]


def params(limit):
    return pltpu.CompilerParams(vmem_limit_bytes=limit * MIB)


def cost(macs, bytes_accessed, exps=0):
    return pl.CostEstimate(
        flops=int(2 * macs), bytes_accessed=int(bytes_accessed), transcendentals=int(exps)
    )


def shaped(rows, width, kind):
    return jax.ShapeDtypeStruct((rows, width), kind)


def line(width):
    return pl.BlockSpec((width,), lambda i: (0,))


def as_row(ref, first=0, count=D):
    return ref[first : first + count].astype(F32).reshape(1, count)


def whole(height, width):
    return pl.BlockSpec((height, width), lambda i: (0, 0))


def embed(tokens, mask_row, fill, gain, shift, weight, order):
    query = lambda i: (jnp.minimum(i, GROUPS - 1), 0)
    other = lambda i: (jnp.maximum(i - GROUPS, 0), 0)
    return pl.pallas_call(
        embed_kernel,
        grid=(3 * GROUPS,),
        in_specs=[
            whole(TILES, D), whole(1, TILES), line(D), line(D), line(D),
            pl.BlockSpec((D, ROWS), lambda i: (0, i)), whole(TILES, TILES),
        ],
        out_specs=[
            whole(D, TILES), whole(TILES, D), whole(8, D),
            pl.BlockSpec((ROWS, TILES), lambda i: (i, 0)),
            pl.BlockSpec((ROWS, QUARTER), query), pl.BlockSpec((ROWS, EIGHTH), query),
            pl.BlockSpec((ROWS, QUARTER), other), pl.BlockSpec((ROWS, QUARTER), other),
        ],
        out_shape=[
            shaped(D, TILES, BF), shaped(TILES, D, BF), shaped(8, D, F32),
            shaped(3 * D, TILES, BF), shaped(D, QUARTER, BF), shaped(D, EIGHTH, BF),
            shaped(2 * D, QUARTER, BF), shaped(2 * D, QUARTER, BF),
        ],
        name="embed",
        compiler_params=params(26),
        cost_estimate=cost(TILES * D * (3 * D + TILES), 20 * MIB),
    )(tokens, mask_row, fill, gain, shift, weight, order)


def forward0_kernel(*refs):
    q_ref, k_ref, v_ref, kt_ref, qt_ref = refs[:5]
    o_ref, l_ref = refs[-2:]

    def body(safe):
        keys = stack(k_ref[...], kt_ref[...]).T
        values = stack(v_ref[...], value_rows(TILES))
        block = 512
        for i in range(TILES // block):
            cut = slice(i * block, (i + 1) * block)
            out, total = attend(keys, values, stack(q_ref[:, cut], qt_ref[:, cut]), safe)
            o_ref[:, cut] = out
            l_ref[0, :, cut] = total

    either_way(largest(q_ref), largest(k_ref), body)


def forward1_kernel(qa_ref, qb_ref, k4_ref, v4_ref, kr_ref, vr_ref, kt_ref, qt_ref, o_ref, l_ref):
    def body(safe):
        for j, q_ref in enumerate((qa_ref, qb_ref)):
            rows = head_rows(j)
            keys = stack(beside(k4_ref[rows], kr_ref[rows]), kt_ref[...]).T
            values = stack(beside(v4_ref[rows], vr_ref[rows]), value_rows(HALF))
            out, total = attend(keys, values, stack(q_ref[...], qt_ref[...]), safe)
            o_ref[rows] = out
            l_ref[j] = total

    either_way(largest(qa_ref) + largest(qb_ref), largest(k4_ref, kr_ref), body)


def forward23_kernel(
    q2_ref, q3a_ref, q3b_ref, k4_ref, v4_ref, k4f_ref, v4f_ref, k8_ref, v8_ref, k8f_ref, v8f_ref,
    kt_ref, qt_ref, z2_ref, z3a_ref, z3b_ref,
):
    table = kt_ref[...]
    zeros = jnp.zeros((16, QUARTER), BF)

    def body(safe):
        for j in range(4):
            rows, outs = head_rows(j), head_rows(j, AUG)
            keys = beside(stack(k4_ref[rows], table), stack(k4f_ref[rows], table)).T
            values = stack(beside(v4_ref[rows], v4f_ref[rows]), value_rows(HALF))
            out, total = attend(keys, values, stack(q2_ref[rows], qt_ref[...]), safe)
            z2_ref[outs] = stack(out, split_rows(total)).astype(BF)
            keys = stack(beside(k8_ref[rows], k8f_ref[rows]), zeros).T
            values = stack(beside(v8_ref[rows], v8f_ref[rows]), value_rows(QUARTER))
            queries = stack(beside(q3a_ref[rows], q3b_ref[rows]), zeros)
            out, total = attend(keys, values, queries, safe)
            packed = stack(out, split_rows(total)).astype(BF)
            z3a_ref[outs] = packed[:, :EIGHTH]
            z3b_ref[outs] = packed[:, EIGHTH:]

    either_way(largest(q2_ref, q3a_ref, q3b_ref), largest(k4_ref, k4f_ref), body)


def merge_kernel(
    o0_ref, l0_ref, o1_ref, l1_ref, z2_ref, z3a_ref, z3b_ref, a_ref, r_ref, l_ref
):
    for j in range(GROUP):
        rows, packs = head_rows(j), head_rows(j, AUG)
        start2, start4, start8 = lanes2(j), lanes4(j), lanes8(j)
        other8 = start4 + EIGHTH - (start8 - start4)

        def own(first, count):
            cut = slice(first, first + count)
            return o0_ref[rows, cut], l0_ref[j, :, cut]

        def pair(first, count):
            cut = slice(first - start2, first - start2 + count)
            return o1_ref[rows, cut], l1_ref[j, :, cut]

        def sent(ref, first, count):
            packed = ref[packs, first : first + count].astype(F32)
            return packed[:HD], jnp.sum(packed[HD : HD + 3], axis=0, keepdims=True)

        def write(first, count, parts):
            peak = parts[0][1]
            for _, total in parts[1:]:
                peak = jnp.maximum(peak, total)
            weights = [jnp.exp2(total - peak) for _, total in parts]
            weight_sum = sum(weights[1:], weights[0])
            inverse = 1.0 / weight_sum
            merged = parts[0][0] * (weights[0] * inverse)
            for (out, _), weight in zip(parts[1:], weights[1:]):
                merged = merged + out * (weight * inverse)
            cut = slice(first, first + count)
            low = merged.astype(BF)
            a_ref[rows, cut] = low
            r_ref[rows, cut] = (merged - low.astype(F32)).astype(BF)
            l_ref[j, :, cut] = peak + jnp.log2(weight_sum)

        far = HALF - start2
        cut = slice(far, far + HALF)
        low = o0_ref[rows, cut].astype(BF)
        a_ref[rows, cut] = low
        r_ref[rows, cut] = (o0_ref[rows, cut] - low.astype(F32)).astype(BF)
        l_ref[j, :, cut] = l0_ref[j, :, cut]
        first = rest2(j)
        write(first, QUARTER, [own(first, QUARTER), pair(first, QUARTER)])
        first = other8
        write(first, EIGHTH, [own(first, EIGHTH), pair(first, EIGHTH), sent(z2_ref, first - start4, EIGHTH)])
        first = start8
        write(
            first, EIGHTH,
            [own(first, EIGHTH), pair(first, EIGHTH), sent(z2_ref, first - start4, EIGHTH),
             sent(z3a_ref, 0, EIGHTH), sent(z3b_ref, 0, EIGHTH)],
        )


def rows_of(height, width, lane_block=None, first=0):
    chosen = lane_block or (lambda i: 0)
    return pl.BlockSpec((height, width), lambda i: (i + first, chosen(i)))


def table_spec(width, index):
    return pl.BlockSpec((16, width), lambda i: (index(i), 0))


def totals_spec(heads, width, first=0):
    return pl.BlockSpec((heads, 1, width), lambda i: (i + first, 0, 0))


def totals_shape(heads, width):
    return jax.ShapeDtypeStruct((heads, 1, width), F32)


PAIRS = HEADS * TILES * TILES


def forward_own(qkv, tables, group, before=()):
    first = group * GROUP
    anywhere = pl.BlockSpec(memory_space=pl.ANY)
    return pl.pallas_call(
        forward0_kernel,
        grid=(GROUP,),
        in_specs=[
            rows_of(HD, TILES, None, first), rows_of(HD, TILES, None, HEADS + first),
            rows_of(HD, TILES, None, 2 * HEADS + first),
            table_spec(TILES, lambda i: i & 7), table_spec(TILES, lambda i: i & 7),
        ] + [anywhere] * len(before),
        out_specs=[rows_of(HD, TILES, None, first), totals_spec(1, TILES, first)],
        out_shape=[shaped(D, TILES, F32), totals_shape(HEADS, TILES)],
        input_output_aliases={5 + i: i for i in range(len(before))},
        name="forward_own",
        compiler_params=params(14),
        cost_estimate=cost(PAIRS // 2 * 600, 4 * MIB, PAIRS // 2),
    )(qkv, qkv, qkv, *tables, *before)


def forward_pair(qkv, kv4, kvr, key_table, query_table):
    pair = rows_of(2 * HD, QUARTER)
    pair_v = rows_of(2 * HD, QUARTER, None, HEADS // 2)
    return pl.pallas_call(
        forward1_kernel,
        grid=(HEADS // 2,),
        in_specs=[
            pl.BlockSpec((HD, HALF), lambda i: (2 * i, 0)),
            pl.BlockSpec((HD, HALF), lambda i: (2 * i + 1, 1)),
            pair, pair_v, pair, pair_v,
            table_spec(HALF, lambda i: i & 3), table_spec(HALF, lambda i: i & 3),
        ],
        out_specs=[rows_of(2 * HD, HALF), totals_spec(2, HALF)],
        out_shape=[shaped(D, HALF, F32), totals_shape(HEADS, HALF)],
        name="forward_pair",
        compiler_params=params(12),
        cost_estimate=cost(PAIRS // 4 * 600, 5 * MIB, PAIRS // 4),
    )(qkv, qkv, kv4, kv4, kvr, kvr, key_table, query_table)


FOUR = HEADS // 4
NEAR = (
    rows_of(4 * HD, QUARTER), rows_of(4 * HD, QUARTER, None, FOUR),
    rows_of(4 * HD, QUARTER), rows_of(4 * HD, QUARTER, None, FOUR),
    rows_of(4 * HD, EIGHTH, lambda i: i & 1), rows_of(4 * HD, EIGHTH, lambda i: i & 1, FOUR),
    rows_of(4 * HD, EIGHTH, lambda i: i & 1), rows_of(4 * HD, EIGHTH, lambda i: i & 1, FOUR),
)


def near_args(own, far):
    return (own, own, far, far, own, own, far, far)


def forward_sent(q2, q3a, q3b, own, far, tables):
    return pl.pallas_call(
        forward23_kernel,
        grid=(FOUR,),
        in_specs=[
            rows_of(4 * HD, QUARTER), rows_of(4 * HD, EIGHTH), rows_of(4 * HD, EIGHTH), *NEAR,
            table_spec(QUARTER, lambda i: i & 1), table_spec(QUARTER, lambda i: i & 1),
        ],
        out_specs=[rows_of(4 * AUG, QUARTER), rows_of(4 * AUG, EIGHTH), rows_of(4 * AUG, EIGHTH)],
        out_shape=[
            shaped(HEADS * AUG, QUARTER, BF), shaped(HEADS * AUG, EIGHTH, BF),
            shaped(HEADS * AUG, EIGHTH, BF),
        ],
        name="forward_sent",
        compiler_params=params(12),
        cost_estimate=cost(PAIRS * 3 // 16 * 600, 4 * MIB, PAIRS * 3 // 16),
    )(q2, q3a, q3b, *near_args(own, far), *tables)


def merge(o0, l0, o1, l1, z2, z3a, z3b):
    return pl.pallas_call(
        merge_kernel,
        grid=(GROUPS,),
        in_specs=[
            rows_of(ROWS, TILES), totals_spec(GROUP, TILES), rows_of(ROWS, HALF), totals_spec(GROUP, HALF),
            rows_of(GROUP * AUG, QUARTER), rows_of(GROUP * AUG, EIGHTH), rows_of(GROUP * AUG, EIGHTH),
        ],
        out_specs=[rows_of(ROWS, TILES), rows_of(ROWS, TILES), totals_spec(GROUP, TILES)],
        out_shape=[shaped(D, TILES, BF), shaped(D, TILES, BF), totals_shape(HEADS, TILES)],
        name="merge",
        compiler_params=params(16),
        cost_estimate=cost(TILES * D * 20, 12 * MIB),
    )(o0, l0, o1, l1, z2, z3a, z3b)


ERFCX = (
    0.25388073921203613, 0.254069447517395, 0.22542551159858704, 0.19709868729114532,
    0.02506333962082863, 0.2244575172662735, -0.2487541288137436, 0.06875886023044586,
)


def gelu_pair(x):
    z = jnp.abs(x) * (0.5**0.5)
    t = 1.0 / (1.0 + 0.45 * z)
    series = jnp.full_like(t, 0.5 * ERFCX[-1])
    for factor in reversed(ERFCX[:-1]):
        series = series * t + 0.5 * factor
    bell = jnp.exp(-z * z)
    tail = bell * (t * series)
    below = jnp.where(x < 0.0, tail, 1.0 - tail)
    return x * below, below + x * (bell * 0.3989422804014327)


CHUNK = 512


def once(height, width):
    return pl.BlockSpec((height, width), lambda i: (0, 0), pipeline_mode=pl.Buffered(1))


def total_rows(value):
    return jnp.sum(value, axis=0, keepdims=True)


def feed_kernel(
    order_ref, turned_ref, rest_ref, total_ref, start_ref, mask_ref, cot_ref,
    proj_bias_ref, down_bias_ref, gain_ref, shift_ref, up_bias_ref, proj_ref, up_ref, down_ref,
    out_ref, mid_ref, g_ref, g4_ref, g8_ref, sum_ref, up_sum_ref, early_out,
    normed, normed_t, attn, middle, final, back, spare, up_block, down_block, proj_block, sems,
):
    step = pl.program_id(0)
    last = pl.num_programs(0) - 1
    ff = down_block.shape[2]
    folds = ff // D
    width = CHUNK
    block = width // folds

    slot = lax.rem(step, 2)

    def up_copy(at):
        lanes = pl.ds(pl.multiple_of(at * width, 128), width)
        here = lax.rem(at, 2)
        return pltpu.make_async_copy(up_block.at[here], early_out.at[:, lanes], sems.at[here])

    def down_copy(at):
        rows = pl.ds(pl.multiple_of(at * block, block), block)
        here = lax.rem(at, 2)
        return pltpu.make_async_copy(
            down_block.at[here], early_out.at[rows, pl.ds(ff + D, ff)], sems.at[2 + here]
        )

    proj_copy = pltpu.make_async_copy(proj_block, early_out.at[:, pl.ds(ff, D)], sems.at[4])

    @pl.when(step >= 2)
    def _():
        up_copy(step - 2).wait()
        down_copy(step - 2).wait()

    @pl.when(step == 0)
    def _():
        low = nt(order_ref[...], turned_ref[...]).astype(BF)
        attn[...] = low
        value = start_ref[...].astype(F32) + nn(low, proj_ref[...]) + as_row(proj_bias_ref)
        middle[...] = value
        low = (normalise(value)[0] * as_row(gain_ref) + as_row(shift_ref)).astype(BF)
        normed[...] = low
        normed_t[...] = low.T
        final[...] = jnp.zeros_like(final)
        back[...] = jnp.zeros_like(back)

    acts, grads = [], []
    up_sum = None
    half = TILES // 2
    for t in range(2):
        rows = slice(t * half, (t + 1) * half)
        pre = nn(normed[rows], up_ref[...]) + as_row(up_bias_ref, 0, width)
        act, slope = gelu_pair(pre)
        act = act.astype(BF)
        acts.append(act)
        grad = (slope * nt(cot_ref[rows], down_ref[...])).astype(BF)
        grads.append(grad)
        part = total_rows(grad.astype(F32))
        up_sum = part if up_sum is None else up_sum + part
        final[rows] += nn(act, down_ref[...])
        back[rows] += nt(grad, up_ref[...])
    up_sum_ref[...] = jnp.broadcast_to(up_sum, (8, width))
    up_block[slot] = nn(normed_t[...], stack(*grads)).astype(BF)
    up_copy(step).start()
    down = tn(stack(*acts), cot_ref[...])
    for k in range(D // 128):
        spare[k] = down[:, k * 128 : (k + 1) * 128]
    for j in range(folds):
        for k in range(D // 128):
            first = j * D + k * 128
            piece = spare[k, pl.ds(j, block, stride=folds), :]
            down_block[slot, :, first : first + 128] = piece.astype(BF)
    down_copy(step).start()

    @pl.when(step == last)
    def _():
        visible = column(1.0 - mask_ref[...].astype(F32), D)
        value = middle[...]
        hat, scale = normalise(value)
        after_value = value + final[...] + as_row(down_bias_ref)
        out_ref[...] = after_value.astype(BF)
        cot = cot_ref[...].astype(F32)
        turned = back[...]
        hat_grad = turned * as_row(gain_ref)
        first = jnp.mean(hat_grad, axis=1, keepdims=True)
        second = jnp.mean(hat_grad * hat, axis=1, keepdims=True)
        mid_grad = cot + scale * (hat_grad - first - hat * second)
        mid_ref[...] = mid_grad
        low = mid_grad.astype(BF)
        proj_block[...] = tn(attn[...], low).astype(BF)
        proj_copy.start()
        for g in range(GROUPS):
            grad = nt(proj_ref[g * ROWS : (g + 1) * ROWS], low).astype(BF)
            grad = nn(grad, order_ref[...])
            for j in range(GROUP):
                h = g * GROUP + j
                rows, packs = head_rows(h), head_rows(h, AUG)
                merged = turned_ref[rows].astype(F32) + rest_ref[rows].astype(F32)
                mine = grad[head_rows(j)]
                packed = stack(mine, split_rows(-total_rows(mine * merged), -total_ref[h])).astype(BF)
                g_ref[packs] = packed
                g4_ref[packs] = packed[:, lanes4(j) : lanes4(j) + QUARTER]
                g8_ref[packs] = packed[:, lanes8(j) : lanes8(j) + EIGHTH]
        sum_ref[...] = stack(
            total_rows(low.astype(F32)), total_rows(cot), total_rows(turned * hat), total_rows(turned),
            total_rows(visible * value * value), total_rows(visible * after_value * after_value),
            jnp.zeros((2, D), F32),
        )
        for at in (step - 1, step):
            up_copy(at).wait()
            down_copy(at).wait()
        proj_copy.wait()


def feed(order, attn_t, rest, total, start, mask_row, cot, vectors, proj, up, down):
    ff = up.shape[1]
    wide = 2 * ff + D
    return pl.pallas_call(
        feed_kernel,
        grid=(ff // CHUNK,),
        in_specs=[
            once(TILES, TILES), once(D, TILES), once(D, TILES),
            pl.BlockSpec((HEADS, 1, TILES), lambda i: (0, 0, 0)), once(TILES, D),
            once(1, TILES), once(TILES, D),
            line(D), line(D), line(D), line(D), pl.BlockSpec((CHUNK,), lambda i: (i,)), once(D, D),
            pl.BlockSpec((D, CHUNK), lambda i: (0, i)), pl.BlockSpec((CHUNK, D), lambda i: (i, 0)),
        ],
        out_specs=[
            once(TILES, D), once(TILES, D), once(HEADS * AUG, TILES), once(HEADS * AUG, QUARTER),
            once(HEADS * AUG, EIGHTH), whole(8, D),
            pl.BlockSpec((8, CHUNK), lambda i: (0, i)), pl.BlockSpec(memory_space=pl.ANY),
        ],
        out_shape=[
            shaped(TILES, D, BF), shaped(TILES, D, F32), shaped(HEADS * AUG, TILES, BF),
            shaped(HEADS * AUG, QUARTER, BF), shaped(HEADS * AUG, EIGHTH, BF), shaped(8, D, F32),
            shaped(8, ff, F32), shaped(D, wide, BF),
        ],
        scratch_shapes=[
            pltpu.VMEM((TILES, D), BF), pltpu.VMEM((D, TILES), BF), pltpu.VMEM((TILES, D), BF),
            pltpu.VMEM((TILES, D), F32), pltpu.VMEM((TILES, D), F32), pltpu.VMEM((TILES, D), F32),
            pltpu.VMEM((D // 128, CHUNK, 128), F32),
            pltpu.VMEM((2, D, CHUNK), BF), pltpu.VMEM((2, CHUNK * D // ff, ff), BF), pltpu.VMEM((D, D), BF),
            pltpu.SemaphoreType.DMA((5,)),
        ],
        name="feed",
        compiler_params=params(62),
        cost_estimate=cost(TILES * D * (6 * ff + 2 * D + TILES), 36 * MIB, TILES * ff),
    )(order, attn_t, rest, total, start, mask_row, cot, *vectors, proj, up, down)


def back_block(keys, values, keys_t, queries, queries_plain, grads):
    probs = jnp.exp2(nn(keys, queries))
    grad_scores = (probs * nn(values, grads)).astype(BF)
    probs = probs.astype(BF)
    grad_q = nn(keys_t, grad_scores) * SCALE
    grad_k = nt(queries_plain, grad_scores) * LN2
    grad_v = nt(grads[:HD], probs)
    return grad_q, grad_k, grad_v


def back1_kernel(
    qa_ref, qb_ref, ga_ref, gb_ref, k4_ref, v4_ref, kr_ref, vr_ref, kt_ref, qt_ref,
    dq_ref, dk_ref, dv_ref, far_ref,
):
    for j, (q_ref, g_ref) in enumerate(((qa_ref, ga_ref), (qb_ref, gb_ref))):
        rows = head_rows(j)
        keys_t = beside(k4_ref[rows], kr_ref[rows])
        keys = stack(keys_t, kt_ref[...]).T
        values = stack(beside(v4_ref[rows], vr_ref[rows]), value_rows(HALF)).T
        grads = g_ref[...]
        queries = stack(q_ref[...], grads[HD:] + qt_ref[...])
        dq, dk, dv = back_block(keys, values, keys_t, queries, q_ref[...], grads)
        dq_ref[rows] = dq
        dk_ref[rows] = dk[:, :QUARTER]
        dv_ref[rows] = dv[:, :QUARTER]
        far_ref[0, rows] = dk[:, QUARTER:].astype(BF)
        far_ref[1, rows] = dv[:, QUARTER:].astype(BF)


def back23_kernel(
    q2_ref, q3a_ref, q3b_ref, g2_ref, g3a_ref, g3b_ref,
    k4_ref, v4_ref, k4f_ref, v4f_ref, k8_ref, v8_ref, k8f_ref, v8f_ref, kt_ref, qt_ref,
    dk1_ref, dv1_ref,
    dq2_ref, dq3a_ref, dq3b_ref, dk_ref, dv_ref, far_ref,
):
    step = pl.program_id(0)
    table = kt_ref[...]
    row = lax.broadcasted_iota(jnp.int32, (16, QUARTER), 0)
    plain = jnp.where((row >= 3) & (row < 6), 1.0, 0.0).astype(BF)
    lane = lax.broadcasted_iota(jnp.int32, (1, QUARTER), 1)
    inside = (lane >= EIGHTH) == ((step & 1) == 1)
    for j in range(4):
        rows, packs = head_rows(j), head_rows(j, AUG)
        keys_t = beside(k4_ref[rows], k4f_ref[rows])
        keys = stack(keys_t, beside(table, table)).T
        values = stack(beside(v4_ref[rows], v4f_ref[rows]), value_rows(HALF)).T
        grads = g2_ref[packs]
        queries = stack(q2_ref[rows], grads[HD:] + qt_ref[...])
        dq, dk4, dv4 = back_block(keys, values, keys_t, queries, q2_ref[rows], grads)
        dq2_ref[rows] = dq.astype(BF)
        keys_t = beside(k8_ref[rows], k8f_ref[rows])
        keys = stack(keys_t, plain).T
        values = stack(beside(v8_ref[rows], v8f_ref[rows]), value_rows(QUARTER)).T
        grads = beside(g3a_ref[packs], g3b_ref[packs])
        plain_q = beside(q3a_ref[rows], q3b_ref[rows])
        queries = stack(plain_q, grads[HD:])
        dq, dk8, dv8 = back_block(keys, values, keys_t, queries, plain_q, grads)
        dq3a_ref[rows] = dq[:, :EIGHTH].astype(BF)
        dq3b_ref[rows] = dq[:, EIGHTH:].astype(BF)
        for kind, own_ref, one_ref, four, eight in (
            (0, dk_ref, dk1_ref, dk4, dk8),
            (1, dv_ref, dv1_ref, dv4, dv8),
        ):
            near, away = eight[:, :EIGHTH], eight[:, EIGHTH:]
            own_ref[rows] = four[:, :QUARTER] + jnp.where(inside, beside(near, near), 0.0)
            extra = four[:, QUARTER:] + jnp.where(inside, beside(away, away), 0.0)
            far_ref[kind, rows] = (one_ref[rows] + extra).astype(BF)


def back0_kernel(*refs):
    q_ref, g_ref, k_ref, v_ref, kt_ref, qt_ref = refs[:6]
    dq_ref, dk_ref, dv_ref = refs[-3:]
    keys_t = k_ref[...]
    keys = stack(keys_t, kt_ref[...]).T
    values = stack(v_ref[...], value_rows(TILES)).T
    block = 512
    dk = dv = None
    for i in range(TILES // block):
        cut = slice(i * block, (i + 1) * block)
        grads = g_ref[:, cut]
        plain_q = q_ref[:, cut]
        queries = stack(plain_q, grads[HD:] + qt_ref[:, cut])
        dq, more_k, more_v = back_block(keys, values, keys_t, queries, plain_q, grads)
        dq_ref[:, cut] = dq.astype(BF)
        dk = more_k if dk is None else dk + more_k
        dv = more_v if dv is None else dv + more_v
    dk_ref[...] = dk.astype(BF)
    dv_ref[...] = dv.astype(BF)


def back_pair(qkv, grads, kv4, kvr, key_table, query_table):
    pair = rows_of(2 * HD, QUARTER)
    pair_v = rows_of(2 * HD, QUARTER, None, HEADS // 2)
    even = lambda height: pl.BlockSpec((height, HALF), lambda i: (2 * i, 0))
    odd = lambda height: pl.BlockSpec((height, HALF), lambda i: (2 * i + 1, 1))
    return pl.pallas_call(
        back1_kernel,
        grid=(HEADS // 2,),
        in_specs=[
            even(HD), odd(HD), even(AUG), odd(AUG), pair, pair_v, pair, pair_v,
            table_spec(HALF, lambda i: i & 3), table_spec(HALF, lambda i: i & 3),
        ],
        out_specs=[
            rows_of(2 * HD, HALF), rows_of(2 * HD, QUARTER), rows_of(2 * HD, QUARTER),
            pl.BlockSpec((2, 2 * HD, QUARTER), lambda i: (0, i, 0)),
        ],
        out_shape=[
            shaped(D, HALF, F32), shaped(D, QUARTER, F32), shaped(D, QUARTER, F32),
            jax.ShapeDtypeStruct((2, D, QUARTER), BF),
        ],
        name="back_pair",
        compiler_params=params(12),
        cost_estimate=cost(PAIRS // 4 * 900, 12 * MIB, PAIRS // 4),
    )(qkv, qkv, grads, grads, kv4, kv4, kvr, kvr, key_table, query_table)


def back_sent(q2, q3a, q3b, g2, g3a, g3b, own, far, tables, dk1, dv1):
    quarter, eighth = rows_of(4 * HD, QUARTER), rows_of(4 * HD, EIGHTH)
    return pl.pallas_call(
        back23_kernel,
        grid=(FOUR,),
        in_specs=[
            quarter, eighth, eighth,
            rows_of(4 * AUG, QUARTER), rows_of(4 * AUG, EIGHTH), rows_of(4 * AUG, EIGHTH), *NEAR,
            table_spec(QUARTER, lambda i: i & 1), table_spec(QUARTER, lambda i: i & 1), quarter, quarter,
        ],
        out_specs=[
            quarter, eighth, eighth, quarter, quarter,
            pl.BlockSpec((2, 4 * HD, QUARTER), lambda i: (0, i, 0)),
        ],
        out_shape=[
            shaped(D, QUARTER, BF), shaped(D, EIGHTH, BF), shaped(D, EIGHTH, BF),
            shaped(D, QUARTER, F32), shaped(D, QUARTER, F32),
            jax.ShapeDtypeStruct((2, D, QUARTER), BF),
        ],
        name="back_sent",
        compiler_params=params(16),
        cost_estimate=cost(PAIRS * 3 // 16 * 900, 12 * MIB, PAIRS * 3 // 16),
    )(q2, q3a, q3b, g2, g3a, g3b, *near_args(own, far), *tables, dk1, dv1)


def back_own(qkv, grads, tables, first, count, before=()):
    full = rows_of(HD, TILES, None, first)
    table = table_spec(TILES, lambda i: (i + first) & 7)
    anywhere = pl.BlockSpec(memory_space=pl.ANY)
    return pl.pallas_call(
        back0_kernel,
        grid=(count,),
        in_specs=[
            full, rows_of(AUG, TILES, None, first), rows_of(HD, TILES, None, HEADS + first),
            rows_of(HD, TILES, None, 2 * HEADS + first), table, table,
        ] + [anywhere] * len(before),
        out_specs=[full, full, full],
        out_shape=[shaped(D, TILES, BF)] * 3,
        input_output_aliases={6 + i: i for i in range(len(before))},
        name="back_own",
        compiler_params=params(16),
        cost_estimate=cost(PAIRS // HEADS * count * 900, 7 * MIB, PAIRS // HEADS * count),
    )(qkv, grads, qkv, qkv, *tables, *before)


def collect_kernel(
    dq_ref, dk_ref, dv_ref, dq1_ref, dq2_ref, dq3a_ref, dq3b_ref, dk4_ref, dv4_ref, far_ref, farr_ref,
    normed_ref, w_ref, grad_ref, back_ref, value_ref,
):
    step = pl.program_id(0)

    def write(base_ref, parts):
        for j in range(GROUP):
            rows = head_rows(j)
            pieces = {
                first: base_ref[rows, first : first + EIGHTH].astype(F32)
                for first in range(0, TILES, EIGHTH)
            }
            for ref, first, count in parts(j):
                for k in range(0, count, EIGHTH):
                    pieces[first + k] = pieces[first + k] + ref[rows, k : k + EIGHTH].astype(F32)
            value_ref[rows] = beside(*(pieces[first] for first in range(0, TILES, EIGHTH))).astype(BF)

    @pl.when(step < GROUPS)
    def _():
        write(
            dq_ref,
            lambda j: (
                (dq1_ref, lanes2(j), HALF), (dq2_ref, lanes4(j), QUARTER),
                (dq3a_ref, lanes8(j), EIGHTH), (dq3b_ref, lanes8(j), EIGHTH),
            ),
        )

    for kind, base_ref, own_ref in ((1, dk_ref, dk4_ref), (2, dv_ref, dv4_ref)):

        @pl.when((step >= kind * GROUPS) & (step < (kind + 1) * GROUPS))
        def _(base_ref=base_ref, own_ref=own_ref):
            write(
                base_ref,
                lambda j: (
                    (own_ref, lanes4(j), QUARTER), (far_ref.at[0], lanes4(j), QUARTER),
                    (farr_ref.at[0], rest2(j), QUARTER),
                ),
            )

    value = value_ref[...]
    grad_ref[...] = nt(normed_ref[...], value).astype(BF)
    back = nn(w_ref[...], value)

    @pl.when(step == 0)
    def _():
        back_ref[...] = back

    @pl.when(step > 0)
    def _():
        back_ref[...] += back


def collect(own, dq1, dq2, dq3a, dq3b, dk4, dv4, far, far_rest, normed, weight):
    def block(width, kind):
        return pl.BlockSpec((ROWS, width), lambda i: (jnp.clip(i - kind * GROUPS, 0, GROUPS - 1), 0))

    away = pl.BlockSpec(
        (1, ROWS, QUARTER),
        lambda i: (jnp.where(i < 2 * GROUPS, 0, 1), jnp.where(i < GROUPS, 0, lax.rem(i, GROUPS)), 0),
    )
    return pl.pallas_call(
        collect_kernel,
        grid=(3 * GROUPS,),
        in_specs=[
            block(TILES, 0), block(TILES, 1), block(TILES, 2),
            block(HALF, 0), block(QUARTER, 0), block(EIGHTH, 0), block(EIGHTH, 0),
            block(QUARTER, 1), block(QUARTER, 2), away, away,
            once(D, TILES), pl.BlockSpec((D, ROWS), lambda i: (0, i)),
        ],
        out_specs=[pl.BlockSpec((D, ROWS), lambda i: (0, i)), whole(D, TILES)],
        out_shape=[shaped(D, 3 * D, BF), shaped(D, TILES, F32)],
        scratch_shapes=[pltpu.VMEM((ROWS, TILES), BF)],
        name="collect",
        compiler_params=params(26),
        cost_estimate=cost(3 * D * TILES * D * 2, 24 * MIB),
    )(*own, dq1, dq2, dq3a, dq3b, dk4, dv4, far, far_rest, normed, weight)


SMALL = 16


def finish_kernel(
    back_ref, order_ref, start_ref, mask_ref, mid_ref, gain_ref,
    masks_ref, feed_ref, up_ref, square_ref, out_ref, small_ref, sums,
):
    step = pl.program_id(0)
    back = nt(order_ref[...], back_ref[...].astype(BF))
    hidden = column(mask_ref[...].astype(F32), D) > 0.5
    hat, scale = normalise(start_ref[...].astype(F32))
    hat_grad = back * as_row(gain_ref)
    first = jnp.mean(hat_grad, axis=1, keepdims=True)
    second = jnp.mean(hat_grad * hat, axis=1, keepdims=True)
    grad = mid_ref[...] + scale * (hat_grad - first - hat * second)
    out_ref[...] = jnp.where(hidden, 0.0, grad).astype(BF)
    more = stack(
        total_rows(back * hat), total_rows(back), total_rows(jnp.where(hidden, grad, 0.0)),
        jnp.zeros((5, D), F32),
    )

    @pl.when(step == 0)
    def _():
        sums[...] = more

    @pl.when(step > 0)
    def _():
        sums[...] += more

    @pl.when(step == pl.num_programs(0) - 1)
    def _():
        width = small_ref.shape[1]
        up = [up_ref[0:1, k * D : (k + 1) * D] for k in range(up_ref.shape[1] // D)]
        rows = stack(sums[0:3], feed_ref[0:6], square_ref[0:1], *up)
        rows = beside(rows, jnp.zeros((rows.shape[0], width - D), F32))
        visible = beside(1.0 - masks_ref[...].astype(F32), jnp.zeros((1, width - TILES), F32))
        rest = jnp.zeros((SMALL - 1 - rows.shape[0], width), F32)
        small_ref[...] = stack(rows, visible, rest).astype(BF)


def finish(back, order, start, mask_row, mid, gain, feed_sums, up_sums, squares):
    block = 256
    ff = up_sums.shape[1]
    part = lambda width: pl.BlockSpec((block, width), lambda i: (i, 0))
    return pl.pallas_call(
        finish_kernel,
        grid=(TILES // block,),
        in_specs=[
            whole(D, TILES), part(TILES), part(D),
            pl.BlockSpec((1, block), lambda i: (0, i)), part(D), line(D),
            whole(1, TILES), whole(8, D), whole(8, ff), whole(8, D),
        ],
        out_specs=[part(D), whole(SMALL, 3 * D)],
        out_shape=[shaped(TILES, D, BF), shaped(SMALL, 3 * D, BF)],
        scratch_shapes=[pltpu.VMEM((8, D), F32)],
        name="finish",
        compiler_params=params(44),
        cost_estimate=cost(TILES * TILES * D, 16 * MIB),
    )(back, order, start, mask_row, mid, gain, mask_row, feed_sums, up_sums, squares)


def exchange(value, axis, mask):
    pairs = [(source, source ^ mask) for source in range(lax.axis_size(axis))]
    return lax.ppermute(value, axis, pairs)


def after(value, *others):
    return lax.optimization_barrier((value,) + others)[0]


def after_all(values, *others):
    return lax.optimization_barrier(tuple(values) + others)[: len(values)]


def swap(value, masks):
    names = tuple(name for name in ("seq", "dp") if name in masks)
    sizes = [lax.axis_size(name) for name in names]

    def partner(index):
        place = []
        for size in reversed(sizes):
            place.append(index % size)
            index //= size
        target = 0
        for size, name, at in zip(sizes, names, reversed(place)):
            target = target * size + (at ^ masks[name])
        return target

    count = int(np.prod(sizes))
    return lax.ppermute(value, names, [(source, partner(source)) for source in range(count)])


def choices(moves):
    for way in range(1, 1 << len(moves)):
        masks = {}
        for k, (axis, bit, _) in enumerate(moves):
            masks.setdefault(axis, 0)
            masks[axis] |= (way >> k & 1) << bit
        yield way, masks


def scatter(value, *moves, plus=None):
    def part(way):
        piece = value
        for k, (axis, bit, dim) in enumerate(moves):
            half = value.shape[dim] // 2
            mine = (lax.axis_index(axis) >> bit & 1) ^ (way >> k & 1)
            piece = lax.dynamic_slice_in_dim(piece, mine * half, half, dim)
        return piece

    pieces = [part(0)] + [swap(part(way), masks) for way, masks in choices(moves)]
    total = pieces[0].astype(F32)
    if plus is not None:
        total = total + plus
    for piece in pieces[1:]:
        total = total + piece.astype(F32)
    return total.astype(BF)


def gather(value, *moves):
    pieces = [value] + [swap(value, masks) for _, masks in choices(moves)]
    stacked = jnp.stack(pieces)
    mine = sum((lax.axis_index(axis) >> bit & 1) << k for k, (axis, bit, _) in enumerate(moves))
    count = len(moves)
    ordered = []
    for place in range(1 << count):
        way = sum((place >> (count - 1 - k) & 1) << k for k in range(count)) ^ mine
        ordered.append(lax.dynamic_index_in_dim(stacked, way, 0, keepdims=False))
    return jnp.concatenate(ordered, axis=0)


def log2_size(axis):
    return (lax.axis_size(axis) - 1).bit_length()


def core_step(value):
    return scatter(value, ("dp", 0, value.ndim - 2))


def near_step(value):
    return scatter(value, ("dp", 1, value.ndim - 2), ("seq", 0, log2_size("seq") - 1))


def far_step(value, zero):
    count = log2_size("seq")
    bits = list(reversed(range(1, count)))
    while bits:
        plus = zero if len(bits) <= 2 else None
        value = scatter(value, *(("seq", bit, count - 1 - bit) for bit in bits[:2]), plus=plus)
        bits = bits[2:]
    return value.reshape(value.shape[-2:])


def in_blocks(grad):
    count = lax.axis_size("seq")
    return grad.reshape((2,) * log2_size("seq") + (grad.shape[0] // count, -1))


def local(
    tokens, tile_mask, cotangent, qkv_weight, proj_weight, proj_bias, up_weight, up_bias,
    down_weight, down_bias, attn_gain, attn_shift, mlp_gain, mlp_shift, mask_vector,
):
    order = order_matrix()
    tables0 = weight_tables(0)
    query_table1 = weight_tables(1)[1]
    key_table1 = weight_tables(1, True)[0]
    tables2 = weight_tables(2)
    seq_count = lax.axis_size("seq")

    normed_t, start, token_squares, qkv, q4, q8, kv4, kvr = embed(
        tokens[0], tile_mask, mask_vector, attn_gain, attn_shift, qkv_weight, order
    )
    q2 = exchange(q4, "seq", 2)
    q3a = exchange(q8, "seq", 4)
    q3b = exchange(q8, "seq", 6)
    kv4_far = exchange(kv4, "seq", 1)
    kvr_far = exchange(after(kvr, kv4_far), "seq", 1)
    own = forward_own(qkv, tables0, 0)
    z2, z3a, z3b = forward_sent(q2, q3a, q3b, kv4, kv4_far, after_all(tables2, own[1]))
    later = after_all(tables0, z2)
    z2 = exchange(z2, "seq", 2)
    z3a = exchange(z3a, "seq", 4)
    z3b = exchange(z3b, "seq", 6)
    own = forward_own(qkv, later, 1, own)
    out1, total1 = forward_pair(qkv, kv4_far, kvr_far, after(key_table1, own[1]), query_table1)
    attn_t, rest, total = merge(*own, out1, total1, z2, z3a, z3b)

    layer_out, grad_mid, grads, g4, g8, feed_sums, up_sums, early = feed(
        order, attn_t, rest, total, start, tile_mask, cotangent[0],
        (proj_bias, down_bias, mlp_gain, mlp_shift, up_bias), proj_weight, up_weight, down_weight,
    )
    early = lax.psum_scatter(early, ("seq", "dp"), scatter_dimension=0, tiled=True)
    g2 = exchange(g4, "seq", 2)
    g3a = exchange(g8, "seq", 4)
    g3b = exchange(g8, "seq", 6)
    dq1, dk1, dv1, far_rest = back_pair(qkv, grads, kv4_far, kvr_far, key_table1, query_table1)
    later = after_all(tables0, far_rest)
    far_rest = exchange(far_rest, "seq", 1)
    part = GROUP // 2
    own_a = back_own(qkv, grads, later, 0, part)
    dq2, dq3a, dq3b, dk4, dv4, far = back_sent(
        q2, q3a, q3b, g2, g3a, g3b, kv4, kv4_far, after_all(tables2, own_a[0]), dk1, dv1
    )
    later = after_all(tables0, far)
    far = exchange(far, "seq", 1)
    dq2 = exchange(dq2, "seq", 2)
    dq3a = exchange(dq3a, "seq", 4)
    dq3b = exchange(dq3b, "seq", 6)
    own = back_own(qkv, grads, later, part, HEADS - part, own_a)
    qkv_grad, back = collect(own, dq1, dq2, dq3a, dq3b, dk4, dv4, far, far_rest, normed_t, qkv_weight)
    chain = in_blocks(qkv_grad)
    seq_dims = chain.shape[:-2]
    chain = core_step(chain)
    tokens_grad, small = finish(
        back, order, start, tile_mask, grad_mid, attn_gain, feed_sums, up_sums, token_squares
    )

    share = D // seq_count
    ff = up_weight.shape[1]
    chain = near_step(chain)
    small = near_step(core_step(jnp.broadcast_to(small, seq_dims + small.shape)))
    dp_moves = (("dp", 0, 0), ("dp", 1, 0))
    chain = far_step(jnp.concatenate([chain, small], axis=-2), early[0, 0].astype(F32) * 0.0)
    both = gather(chain, *dp_moves)
    early = gather(early, *reversed(dp_moves))
    quarter, inner = share // 4, chain.shape[0]
    qkv_grad, small = (
        jnp.concatenate([both[k * inner + first : k * inner + last] for k in range(4)])
        for first, last in ((0, quarter), (quarter, inner))
    )
    qkv_grad = qkv_grad.astype(F32)
    small = small.astype(F32)
    mine = lax.axis_index("seq") * share
    vectors = lax.dynamic_slice_in_dim(small[:7, :D], mine, share, 1)
    gain_grad, shift_grad, mask_grad, proj_bias_grad, down_bias_grad, gain2_grad, shift2_grad = (
        vectors[k] for k in range(7)
    )
    first = 10
    last = first + ff // D
    up_bias_grad = lax.dynamic_slice_in_dim(
        small[first:last, :D].reshape(ff), lax.axis_index("seq") * (ff // seq_count), ff // seq_count
    )
    middle_squares, final_squares, token_squares, count = (
        jnp.sum(small[k]) for k in (7, 8, 9, last)
    )
    stream_rms = jnp.sqrt(jnp.stack([token_squares, middle_squares, final_squares]) / (count * D))
    early = early.astype(F32)
    up_grad, proj_grad = early[:, :ff], early[:, ff : ff + D]
    down_grad = early[:, ff + D :].reshape(-1, D)
    return (
        layer_out[None], tokens_grad[None], qkv_grad, proj_grad, proj_bias_grad, up_grad, up_bias_grad,
        down_grad, down_bias_grad, gain_grad, shift_grad, gain2_grad, shift2_grad, mask_grad, stream_rms,
    )


def solution(mesh):
    rows = P("dp", "seq", None)
    in_specs = (rows, P("dp", "seq"), rows) + (P(),) * 12
    matrix, vector = P("seq", None), P("seq")
    out_specs = (
        rows, rows, matrix, matrix, vector, matrix, vector, matrix,
        vector, vector, vector, vector, vector, vector, P(),
    )
    return jax.shard_map(local, mesh=mesh, in_specs=in_specs, out_specs=out_specs, check_vma=False)
```

```python
import functools

import numpy as np
import jax
import jax.numpy as jnp
from jax import lax
from jax.experimental import pallas as pl
from jax.experimental.pallas import tpu as pltpu
from jax.sharding import PartitionSpec as P

HEADS = 16
HD = 48
AUG = 64
TILES = 1024
EPS = 1e-06
FILL = -1e30
LN2 = float(np.log(2.0))
SCALE = HD**-0.5
QSCALE = SCALE / LN2
BF = jnp.bfloat16
F32 = jnp.float32


def nn(a, b):
    return lax.dot_general(a, b, (((1,), (0,)), ((), ())), preferred_element_type=F32)


def nt(a, b):
    return lax.dot_general(a, b, (((1,), (1,)), ((), ())), preferred_element_type=F32)


def tn(a, b):
    return lax.dot_general(a, b, (((0,), (0,)), ((), ())), preferred_element_type=F32)


GROUP = 8
GROUPS = HEADS // GROUP
D = HEADS * HD
ROWS = GROUP * HD
HALF, QUARTER, EIGHTH = TILES // 2, TILES // 4, TILES // 8
MIB = 1024 * 1024


def place_of(tile):
    return (tile & 1) * HALF + (tile >> 1 & 1) * QUARTER + (tile >> 2 & 1) * EIGHTH + (tile >> 3)


def order_matrix():
    tile = np.arange(TILES)
    matrix = np.zeros((TILES, TILES), np.float32)
    matrix[tile, place_of(tile)] = 1.0
    return jnp.asarray(matrix.astype(jnp.bfloat16))


def lanes2(h):
    return (h & 1) * HALF


def lanes4(h):
    return lanes2(h) + (h >> 1 & 1) * QUARTER


def rest2(h):
    return lanes2(h) + (1 - (h >> 1 & 1)) * QUARTER


def lanes8(h):
    return lanes4(h) + (h >> 2 & 1) * EIGHTH


def weight_tables(level, compact=False):
    count = TILES >> level
    classes = 8 >> level
    totals = {0: [2.0, 3.0, 4.0], 1: [2.0, 3.0], 2: [2.0]}[level]
    lane = np.arange(count)
    key_rows = np.zeros((classes, 16, count), np.float32)
    query_rows = np.zeros((classes, 16, count), np.float32)
    key_rows[:, 3:6] = 1.0
    for c in range(classes):
        inside = np.ones(count, bool)
        before = 1.0
        for i, total in enumerate(totals):
            bit = (lane >> (9 - level - i)) & 1
            wanted = 0 if compact and i == 0 else c >> i & 1
            inside = inside & (bit == wanted)
            step = np.log2(total) - np.log2(before)
            before = total
            high = np.float32(np.asarray(step, np.float32).astype(jnp.bfloat16))
            key_rows[c, 6 + 2 * i] = inside
            key_rows[c, 7 + 2 * i] = inside
            query_rows[c, 6 + 2 * i] = inside * high
            query_rows[c, 7 + 2 * i] = inside * (step - high)
    shape = (classes * 16, count)
    return (
        jnp.asarray(key_rows.reshape(shape).astype(jnp.bfloat16)),
        jnp.asarray(query_rows.reshape(shape).astype(jnp.bfloat16)),
    )


def value_rows(count):
    row = lax.broadcasted_iota(jnp.int32, (16, count), 0)
    return jnp.where(row < 3, 1.0, 0.0).astype(BF)


def stack(*parts):
    return jnp.concatenate(parts, axis=0)


def beside(*parts):
    return jnp.concatenate(parts, axis=1)


def head_rows(j, height=HD):
    return slice(j * height, (j + 1) * height)


SAFE = 60.0


def attend(keys, values, queries, safe):
    scores = nn(keys, queries)
    if safe:
        probs = jnp.exp2(scores).astype(BF)
    else:
        peak = jnp.max(scores, axis=0, keepdims=True)
        probs = jnp.exp2(scores - peak).astype(BF)
    out = nn(values, probs)
    total = out[HD : HD + 1]
    level = jnp.log2(total)
    return out[:HD] / total, level if safe else peak + level


def largest(*refs):
    count = refs[0].shape[0] // HD
    squares = [jnp.square(ref[...].astype(F32)) for ref in refs]
    result = []
    for j in range(count):
        rows = [jnp.sum(square[head_rows(j)], axis=0, keepdims=True) for square in squares]
        top = jnp.max(rows[0])
        for row in rows[1:]:
            top = jnp.maximum(top, jnp.max(row))
        result.append(top)
    return result


def either_way(query_tops, key_tops, body):
    bound = query_tops[0] * key_tops[0]
    for query_top, key_top in zip(query_tops[1:], key_tops[1:]):
        bound = jnp.maximum(bound, query_top * key_top)
    safe = bound < SAFE * SAFE

    @pl.when(safe)
    def _():
        body(True)

    @pl.when(jnp.logical_not(safe))
    def _():
        body(False)


def split3(value):
    high = value.astype(BF).astype(F32)
    rest = value - high
    mid = rest.astype(BF).astype(F32)
    return high, mid, rest - mid


def split_rows(*values):
    row = lax.broadcasted_iota(jnp.int32, (16, values[0].shape[1]), 0)
    packed = jnp.zeros((16, values[0].shape[1]), F32)
    for i, value in enumerate(values):
        for k, piece in enumerate(split3(value)):
            packed = jnp.where(row == 3 * i + k, piece, packed)
    return packed


def column(row, width):
    turned = jnp.broadcast_to(row, (128, row.shape[1])).T
    return jnp.concatenate([turned] * (width // 128), axis=1)


def normalise(value):
    average = jnp.mean(value, axis=1, keepdims=True)
    centred = value - average
    spread = jnp.mean(centred * centred, axis=1, keepdims=True)
    scale = lax.rsqrt(spread + EPS)
    return centred * scale, scale


def embed_kernel(
    tok_ref, mask_ref, fill_ref, gain_ref, shift_ref, w_ref, order_ref,
    normed_ref, start_ref, square_ref, qkv_ref, q4_ref, q8_ref, kv4_ref, kvr_ref,
):
    step = pl.program_id(0)

    @pl.when(step == 0)
    def _():
        hidden = column(mask_ref[...].astype(F32), D) > 0.5
        rows = tok_ref[...].astype(F32)
        start = jnp.where(hidden, as_row(fill_ref), rows)
        start_ref[...] = start.astype(BF)
        squares = jnp.where(hidden, 0.0, rows * rows)
        square_ref[...] = jnp.broadcast_to(jnp.sum(squares, axis=0, keepdims=True), (8, D))
        normed = normalise(start)[0] * as_row(gain_ref) + as_row(shift_ref)
        normed_ref[...] = tn(normed.astype(BF), order_ref[...]).astype(BF)

    value = tn(w_ref[...], normed_ref[...])

    @pl.when(step < GROUPS)
    def _():
        low = (value * QSCALE).astype(BF)
        qkv_ref[...] = low
        for j in range(GROUP):
            rows = head_rows(j)
            q4_ref[rows] = low[rows, lanes4(j) : lanes4(j) + QUARTER]
            q8_ref[rows] = low[rows, lanes8(j) : lanes8(j) + EIGHTH]

    @pl.when(step >= GROUPS)
    def _():
        low = value.astype(BF)
        qkv_ref[...] = low
        for j in range(GROUP):
            rows = head_rows(j)
            kv4_ref[rows] = low[rows, lanes4(j) : lanes4(j) + QUARTER]
            kvr_ref[rows] = low[rows, rest2(j) : rest2(j) + QUARTER]


def params(limit):
    return pltpu.CompilerParams(vmem_limit_bytes=limit * MIB)


def cost(macs, bytes_accessed, exps=0):
    return pl.CostEstimate(
        flops=int(2 * macs), bytes_accessed=int(bytes_accessed), transcendentals=int(exps)
    )


def shaped(rows, width, kind):
    return jax.ShapeDtypeStruct((rows, width), kind)


def line(width):
    return pl.BlockSpec((width,), lambda i: (0,))


def as_row(ref, first=0, count=D):
    return ref[first : first + count].astype(F32).reshape(1, count)


def whole(height, width):
    return pl.BlockSpec((height, width), lambda i: (0, 0))


def embed(tokens, mask_row, fill, gain, shift, weight, order):
    query = lambda i: (jnp.minimum(i, GROUPS - 1), 0)
    other = lambda i: (jnp.maximum(i - GROUPS, 0), 0)
    return pl.pallas_call(
        embed_kernel,
        grid=(3 * GROUPS,),
        in_specs=[
            whole(TILES, D), whole(1, TILES), line(D), line(D), line(D),
            pl.BlockSpec((D, ROWS), lambda i: (0, i)), whole(TILES, TILES),
        ],
        out_specs=[
            whole(D, TILES), whole(TILES, D), whole(8, D),
            pl.BlockSpec((ROWS, TILES), lambda i: (i, 0)),
            pl.BlockSpec((ROWS, QUARTER), query), pl.BlockSpec((ROWS, EIGHTH), query),
            pl.BlockSpec((ROWS, QUARTER), other), pl.BlockSpec((ROWS, QUARTER), other),
        ],
        out_shape=[
            shaped(D, TILES, BF), shaped(TILES, D, BF), shaped(8, D, F32),
            shaped(3 * D, TILES, BF), shaped(D, QUARTER, BF), shaped(D, EIGHTH, BF),
            shaped(2 * D, QUARTER, BF), shaped(2 * D, QUARTER, BF),
        ],
        name="embed",
        compiler_params=params(26),
        cost_estimate=cost(TILES * D * (3 * D + TILES), 20 * MIB),
    )(tokens, mask_row, fill, gain, shift, weight, order)


def forward0_kernel(*refs):
    q_ref, k_ref, v_ref, kt_ref, qt_ref = refs[:5]
    o_ref, l_ref = refs[-2:]

    def body(safe):
        keys = stack(k_ref[...], kt_ref[...]).T
        values = stack(v_ref[...], value_rows(TILES))
        block = 512
        for i in range(TILES // block):
            cut = slice(i * block, (i + 1) * block)
            out, total = attend(keys, values, stack(q_ref[:, cut], qt_ref[:, cut]), safe)
            o_ref[:, cut] = out
            l_ref[0, :, cut] = total

    either_way(largest(q_ref), largest(k_ref), body)


def forward1_kernel(qa_ref, qb_ref, k4_ref, v4_ref, kr_ref, vr_ref, kt_ref, qt_ref, o_ref, l_ref):
    def body(safe):
        for j, q_ref in enumerate((qa_ref, qb_ref)):
            rows = head_rows(j)
            keys = stack(beside(k4_ref[rows], kr_ref[rows]), kt_ref[...]).T
            values = stack(beside(v4_ref[rows], vr_ref[rows]), value_rows(HALF))
            out, total = attend(keys, values, stack(q_ref[...], qt_ref[...]), safe)
            o_ref[rows] = out
            l_ref[j] = total

    either_way(largest(qa_ref) + largest(qb_ref), largest(k4_ref, kr_ref), body)


def forward23_kernel(
    q2_ref, q3a_ref, q3b_ref, k4_ref, v4_ref, k4f_ref, v4f_ref, k8_ref, v8_ref, k8f_ref, v8f_ref,
    kt_ref, qt_ref, z2_ref, z3a_ref, z3b_ref,
):
    table = kt_ref[...]
    zeros = jnp.zeros((16, QUARTER), BF)

    def body(safe):
        for j in range(4):
            rows, outs = head_rows(j), head_rows(j, AUG)
            keys = beside(stack(k4_ref[rows], table), stack(k4f_ref[rows], table)).T
            values = stack(beside(v4_ref[rows], v4f_ref[rows]), value_rows(HALF))
            out, total = attend(keys, values, stack(q2_ref[rows], qt_ref[...]), safe)
            z2_ref[outs] = stack(out, split_rows(total)).astype(BF)
            keys = stack(beside(k8_ref[rows], k8f_ref[rows]), zeros).T
            values = stack(beside(v8_ref[rows], v8f_ref[rows]), value_rows(QUARTER))
            queries = stack(beside(q3a_ref[rows], q3b_ref[rows]), zeros)
            out, total = attend(keys, values, queries, safe)
            packed = stack(out, split_rows(total)).astype(BF)
            z3a_ref[outs] = packed[:, :EIGHTH]
            z3b_ref[outs] = packed[:, EIGHTH:]

    either_way(largest(q2_ref, q3a_ref, q3b_ref), largest(k4_ref, k4f_ref), body)


def merge_kernel(
    o0_ref, l0_ref, o1_ref, l1_ref, z2_ref, z3a_ref, z3b_ref, a_ref, r_ref, l_ref
):
    for j in range(GROUP):
        rows, packs = head_rows(j), head_rows(j, AUG)
        start2, start4, start8 = lanes2(j), lanes4(j), lanes8(j)
        other8 = start4 + EIGHTH - (start8 - start4)

        def own(first, count):
            cut = slice(first, first + count)
            return o0_ref[rows, cut], l0_ref[j, :, cut]

        def pair(first, count):
            cut = slice(first - start2, first - start2 + count)
            return o1_ref[rows, cut], l1_ref[j, :, cut]

        def sent(ref, first, count):
            packed = ref[packs, first : first + count].astype(F32)
            return packed[:HD], jnp.sum(packed[HD : HD + 3], axis=0, keepdims=True)

        def write(first, count, parts):
            peak = parts[0][1]
            for _, total in parts[1:]:
                peak = jnp.maximum(peak, total)
            weights = [jnp.exp2(total - peak) for _, total in parts]
            weight_sum = sum(weights[1:], weights[0])
            inverse = 1.0 / weight_sum
            merged = parts[0][0] * (weights[0] * inverse)
            for (out, _), weight in zip(parts[1:], weights[1:]):
                merged = merged + out * (weight * inverse)
            cut = slice(first, first + count)
            low = merged.astype(BF)
            a_ref[rows, cut] = low
            r_ref[rows, cut] = (merged - low.astype(F32)).astype(BF)
            l_ref[j, :, cut] = peak + jnp.log2(weight_sum)

        far = HALF - start2
        cut = slice(far, far + HALF)
        low = o0_ref[rows, cut].astype(BF)
        a_ref[rows, cut] = low
        r_ref[rows, cut] = (o0_ref[rows, cut] - low.astype(F32)).astype(BF)
        l_ref[j, :, cut] = l0_ref[j, :, cut]
        first = rest2(j)
        write(first, QUARTER, [own(first, QUARTER), pair(first, QUARTER)])
        first = other8
        write(first, EIGHTH, [own(first, EIGHTH), pair(first, EIGHTH), sent(z2_ref, first - start4, EIGHTH)])
        first = start8
        write(
            first, EIGHTH,
            [own(first, EIGHTH), pair(first, EIGHTH), sent(z2_ref, first - start4, EIGHTH),
             sent(z3a_ref, 0, EIGHTH), sent(z3b_ref, 0, EIGHTH)],
        )


def rows_of(height, width, lane_block=None, first=0):
    chosen = lane_block or (lambda i: 0)
    return pl.BlockSpec((height, width), lambda i: (i + first, chosen(i)))


def table_spec(width, index):
    return pl.BlockSpec((16, width), lambda i: (index(i), 0))


def totals_spec(heads, width, first=0):
    return pl.BlockSpec((heads, 1, width), lambda i: (i + first, 0, 0))


def totals_shape(heads, width):
    return jax.ShapeDtypeStruct((heads, 1, width), F32)


PAIRS = HEADS * TILES * TILES


def forward_own(qkv, tables, group, before=()):
    first = group * GROUP
    anywhere = pl.BlockSpec(memory_space=pl.ANY)
    return pl.pallas_call(
        forward0_kernel,
        grid=(GROUP,),
        in_specs=[
            rows_of(HD, TILES, None, first), rows_of(HD, TILES, None, HEADS + first),
            rows_of(HD, TILES, None, 2 * HEADS + first),
            table_spec(TILES, lambda i: i & 7), table_spec(TILES, lambda i: i & 7),
        ] + [anywhere] * len(before),
        out_specs=[rows_of(HD, TILES, None, first), totals_spec(1, TILES, first)],
        out_shape=[shaped(D, TILES, F32), totals_shape(HEADS, TILES)],
        input_output_aliases={5 + i: i for i in range(len(before))},
        name="forward_own",
        compiler_params=params(14),
        cost_estimate=cost(PAIRS // 2 * 600, 4 * MIB, PAIRS // 2),
    )(qkv, qkv, qkv, *tables, *before)


def forward_pair(qkv, kv4, kvr, key_table, query_table):
    pair = rows_of(2 * HD, QUARTER)
    pair_v = rows_of(2 * HD, QUARTER, None, HEADS // 2)
    return pl.pallas_call(
        forward1_kernel,
        grid=(HEADS // 2,),
        in_specs=[
            pl.BlockSpec((HD, HALF), lambda i: (2 * i, 0)),
            pl.BlockSpec((HD, HALF), lambda i: (2 * i + 1, 1)),
            pair, pair_v, pair, pair_v,
            table_spec(HALF, lambda i: i & 3), table_spec(HALF, lambda i: i & 3),
        ],
        out_specs=[rows_of(2 * HD, HALF), totals_spec(2, HALF)],
        out_shape=[shaped(D, HALF, F32), totals_shape(HEADS, HALF)],
        name="forward_pair",
        compiler_params=params(12),
        cost_estimate=cost(PAIRS // 4 * 600, 5 * MIB, PAIRS // 4),
    )(qkv, qkv, kv4, kv4, kvr, kvr, key_table, query_table)


FOUR = HEADS // 4
NEAR = (
    rows_of(4 * HD, QUARTER), rows_of(4 * HD, QUARTER, None, FOUR),
    rows_of(4 * HD, QUARTER), rows_of(4 * HD, QUARTER, None, FOUR),
    rows_of(4 * HD, EIGHTH, lambda i: i & 1), rows_of(4 * HD, EIGHTH, lambda i: i & 1, FOUR),
    rows_of(4 * HD, EIGHTH, lambda i: i & 1), rows_of(4 * HD, EIGHTH, lambda i: i & 1, FOUR),
)


def near_args(own, far):
    return (own, own, far, far, own, own, far, far)


def forward_sent(q2, q3a, q3b, own, far, tables):
    return pl.pallas_call(
        forward23_kernel,
        grid=(FOUR,),
        in_specs=[
            rows_of(4 * HD, QUARTER), rows_of(4 * HD, EIGHTH), rows_of(4 * HD, EIGHTH), *NEAR,
            table_spec(QUARTER, lambda i: i & 1), table_spec(QUARTER, lambda i: i & 1),
        ],
        out_specs=[rows_of(4 * AUG, QUARTER), rows_of(4 * AUG, EIGHTH), rows_of(4 * AUG, EIGHTH)],
        out_shape=[
            shaped(HEADS * AUG, QUARTER, BF), shaped(HEADS * AUG, EIGHTH, BF),
            shaped(HEADS * AUG, EIGHTH, BF),
        ],
        name="forward_sent",
        compiler_params=params(12),
        cost_estimate=cost(PAIRS * 3 // 16 * 600, 4 * MIB, PAIRS * 3 // 16),
    )(q2, q3a, q3b, *near_args(own, far), *tables)


def merge(o0, l0, o1, l1, z2, z3a, z3b):
    return pl.pallas_call(
        merge_kernel,
        grid=(GROUPS,),
        in_specs=[
            rows_of(ROWS, TILES), totals_spec(GROUP, TILES), rows_of(ROWS, HALF), totals_spec(GROUP, HALF),
            rows_of(GROUP * AUG, QUARTER), rows_of(GROUP * AUG, EIGHTH), rows_of(GROUP * AUG, EIGHTH),
        ],
        out_specs=[rows_of(ROWS, TILES), rows_of(ROWS, TILES), totals_spec(GROUP, TILES)],
        out_shape=[shaped(D, TILES, BF), shaped(D, TILES, BF), totals_shape(HEADS, TILES)],
        name="merge",
        compiler_params=params(16),
        cost_estimate=cost(TILES * D * 20, 12 * MIB),
    )(o0, l0, o1, l1, z2, z3a, z3b)


ERFCX = (
    0.25388073921203613, 0.254069447517395, 0.22542551159858704, 0.19709868729114532,
    0.02506333962082863, 0.2244575172662735, -0.2487541288137436, 0.06875886023044586,
)


def gelu_pair(x):
    z = jnp.abs(x) * (0.5**0.5)
    t = 1.0 / (1.0 + 0.45 * z)
    series = jnp.full_like(t, 0.5 * ERFCX[-1])
    for factor in reversed(ERFCX[:-1]):
        series = series * t + 0.5 * factor
    bell = jnp.exp(-z * z)
    tail = bell * (t * series)
    below = jnp.where(x < 0.0, tail, 1.0 - tail)
    return x * below, below + x * (bell * 0.3989422804014327)


CHUNK = 512


def once(height, width):
    return pl.BlockSpec((height, width), lambda i: (0, 0), pipeline_mode=pl.Buffered(1))


def total_rows(value):
    return jnp.sum(value, axis=0, keepdims=True)


def feed_kernel(
    order_ref, turned_ref, rest_ref, total_ref, start_ref, mask_ref, cot_ref,
    proj_bias_ref, down_bias_ref, gain_ref, shift_ref, up_bias_ref, proj_ref, up_ref, down_ref,
    out_ref, mid_ref, g_ref, g4_ref, g8_ref, sum_ref, up_sum_ref, proj_out, early_out,
    normed, normed_t, attn, middle, final, back, spare, up_block, down_block, sems,
):
    step = pl.program_id(0)
    last = pl.num_programs(0) - 1
    ff = down_block.shape[2]
    folds = ff // D
    width = CHUNK
    block = width // folds

    slot = lax.rem(step, 2)

    def up_copy(at):
        lanes = pl.ds(pl.multiple_of(at * width, 128), width)
        here = lax.rem(at, 2)
        return pltpu.make_async_copy(up_block.at[here], early_out.at[:, lanes], sems.at[here])

    def down_copy(at):
        rows = pl.ds(pl.multiple_of(at * block, block), block)
        here = lax.rem(at, 2)
        return pltpu.make_async_copy(
            down_block.at[here], early_out.at[rows, pl.ds(ff, ff)], sems.at[2 + here]
        )

    @pl.when(step >= 2)
    def _():
        up_copy(step - 2).wait()
        down_copy(step - 2).wait()

    @pl.when(step == 0)
    def _():
        low = nt(order_ref[...], turned_ref[...]).astype(BF)
        attn[...] = low
        value = start_ref[...].astype(F32) + nn(low, proj_ref[...]) + as_row(proj_bias_ref)
        middle[...] = value
        low = (normalise(value)[0] * as_row(gain_ref) + as_row(shift_ref)).astype(BF)
        normed[...] = low
        normed_t[...] = low.T
        final[...] = jnp.zeros_like(final)
        back[...] = jnp.zeros_like(back)

    acts, grads = [], []
    up_sum = None
    half = TILES // 2
    for t in range(2):
        rows = slice(t * half, (t + 1) * half)
        pre = nn(normed[rows], up_ref[...]) + as_row(up_bias_ref, 0, width)
        act, slope = gelu_pair(pre)
        act = act.astype(BF)
        acts.append(act)
        grad = (slope * nt(cot_ref[rows], down_ref[...])).astype(BF)
        grads.append(grad)
        part = total_rows(grad.astype(F32))
        up_sum = part if up_sum is None else up_sum + part
        final[rows] += nn(act, down_ref[...])
        back[rows] += nt(grad, up_ref[...])
    up_sum_ref[...] = jnp.broadcast_to(up_sum, (8, width))
    up_block[slot] = nn(normed_t[...], stack(*grads)).astype(BF)
    up_copy(step).start()
    down = tn(stack(*acts), cot_ref[...])
    for k in range(D // 128):
        spare[k] = down[:, k * 128 : (k + 1) * 128]
    for j in range(folds):
        for k in range(D // 128):
            first = j * D + k * 128
            piece = spare[k, pl.ds(j, block, stride=folds), :]
            down_block[slot, :, first : first + 128] = piece.astype(BF)
    down_copy(step).start()

    @pl.when(step == last)
    def _():
        visible = column(1.0 - mask_ref[...].astype(F32), D)
        value = middle[...]
        hat, scale = normalise(value)
        after_value = value + final[...] + as_row(down_bias_ref)
        out_ref[...] = after_value.astype(BF)
        cot = cot_ref[...].astype(F32)
        turned = back[...]
        hat_grad = turned * as_row(gain_ref)
        first = jnp.mean(hat_grad, axis=1, keepdims=True)
        second = jnp.mean(hat_grad * hat, axis=1, keepdims=True)
        mid_grad = cot + scale * (hat_grad - first - hat * second)
        mid_ref[...] = mid_grad
        low = mid_grad.astype(BF)
        proj_out[...] = tn(attn[...], low).astype(BF)
        for g in range(GROUPS):
            grad = nt(proj_ref[g * ROWS : (g + 1) * ROWS], low).astype(BF)
            grad = nn(grad, order_ref[...])
            for j in range(GROUP):
                h = g * GROUP + j
                rows, packs = head_rows(h), head_rows(h, AUG)
                merged = turned_ref[rows].astype(F32) + rest_ref[rows].astype(F32)
                mine = grad[head_rows(j)]
                packed = stack(mine, split_rows(-total_rows(mine * merged), -total_ref[h])).astype(BF)
                g_ref[packs] = packed
                g4_ref[packs] = packed[:, lanes4(j) : lanes4(j) + QUARTER]
                g8_ref[packs] = packed[:, lanes8(j) : lanes8(j) + EIGHTH]
        sum_ref[...] = stack(
            total_rows(low.astype(F32)), total_rows(cot), total_rows(turned * hat), total_rows(turned),
            total_rows(visible * value * value), total_rows(visible * after_value * after_value),
            jnp.zeros((2, D), F32),
        )
        for at in (step - 1, step):
            up_copy(at).wait()
            down_copy(at).wait()


def feed(order, attn_t, rest, total, start, mask_row, cot, vectors, proj, up, down):
    ff = up.shape[1]
    wide = 2 * ff
    return pl.pallas_call(
        feed_kernel,
        grid=(ff // CHUNK,),
        in_specs=[
            once(TILES, TILES), once(D, TILES), once(D, TILES),
            pl.BlockSpec((HEADS, 1, TILES), lambda i: (0, 0, 0)), once(TILES, D),
            once(1, TILES), once(TILES, D),
            line(D), line(D), line(D), line(D), pl.BlockSpec((CHUNK,), lambda i: (i,)), once(D, D),
            pl.BlockSpec((D, CHUNK), lambda i: (0, i)), pl.BlockSpec((CHUNK, D), lambda i: (i, 0)),
        ],
        out_specs=[
            once(TILES, D), once(TILES, D), once(HEADS * AUG, TILES), once(HEADS * AUG, QUARTER),
            once(HEADS * AUG, EIGHTH), whole(8, D),
            pl.BlockSpec((8, CHUNK), lambda i: (0, i)), once(D, D), pl.BlockSpec(memory_space=pl.ANY),
        ],
        out_shape=[
            shaped(TILES, D, BF), shaped(TILES, D, F32), shaped(HEADS * AUG, TILES, BF),
            shaped(HEADS * AUG, QUARTER, BF), shaped(HEADS * AUG, EIGHTH, BF), shaped(8, D, F32),
            shaped(8, ff, F32), shaped(D, D, BF), shaped(D, wide, BF),
        ],
        scratch_shapes=[
            pltpu.VMEM((TILES, D), BF), pltpu.VMEM((D, TILES), BF), pltpu.VMEM((TILES, D), BF),
            pltpu.VMEM((TILES, D), F32), pltpu.VMEM((TILES, D), F32), pltpu.VMEM((TILES, D), F32),
            pltpu.VMEM((D // 128, CHUNK, 128), F32),
            pltpu.VMEM((2, D, CHUNK), BF), pltpu.VMEM((2, CHUNK * D // ff, ff), BF),
            pltpu.SemaphoreType.DMA((4,)),
        ],
        name="feed",
        compiler_params=params(62),
        cost_estimate=cost(TILES * D * (6 * ff + 2 * D + TILES), 36 * MIB, TILES * ff),
    )(order, attn_t, rest, total, start, mask_row, cot, *vectors, proj, up, down)


def back_block(keys, values, keys_t, queries, queries_plain, grads):
    probs = jnp.exp2(nn(keys, queries))
    grad_scores = (probs * nn(values, grads)).astype(BF)
    probs = probs.astype(BF)
    grad_q = nn(keys_t, grad_scores) * SCALE
    grad_k = nt(queries_plain, grad_scores) * LN2
    grad_v = nt(grads[:HD], probs)
    return grad_q, grad_k, grad_v


def back1_kernel(
    qa_ref, qb_ref, ga_ref, gb_ref, k4_ref, v4_ref, kr_ref, vr_ref, kt_ref, qt_ref,
    dq_ref, dk_ref, dv_ref, far_ref,
):
    for j, (q_ref, g_ref) in enumerate(((qa_ref, ga_ref), (qb_ref, gb_ref))):
        rows = head_rows(j)
        keys_t = beside(k4_ref[rows], kr_ref[rows])
        keys = stack(keys_t, kt_ref[...]).T
        values = stack(beside(v4_ref[rows], vr_ref[rows]), value_rows(HALF)).T
        grads = g_ref[...]
        queries = stack(q_ref[...], grads[HD:] + qt_ref[...])
        dq, dk, dv = back_block(keys, values, keys_t, queries, q_ref[...], grads)
        dq_ref[rows] = dq
        dk_ref[rows] = dk[:, :QUARTER]
        dv_ref[rows] = dv[:, :QUARTER]
        far_ref[0, rows] = dk[:, QUARTER:].astype(BF)
        far_ref[1, rows] = dv[:, QUARTER:].astype(BF)


def back23_kernel(
    q2_ref, q3a_ref, q3b_ref, g2_ref, g3a_ref, g3b_ref,
    k4_ref, v4_ref, k4f_ref, v4f_ref, k8_ref, v8_ref, k8f_ref, v8f_ref, kt_ref, qt_ref,
    dk1_ref, dv1_ref,
    dq2_ref, dq3a_ref, dq3b_ref, dk_ref, dv_ref, far_ref,
):
    step = pl.program_id(0)
    table = kt_ref[...]
    row = lax.broadcasted_iota(jnp.int32, (16, QUARTER), 0)
    plain = jnp.where((row >= 3) & (row < 6), 1.0, 0.0).astype(BF)
    lane = lax.broadcasted_iota(jnp.int32, (1, QUARTER), 1)
    inside = (lane >= EIGHTH) == ((step & 1) == 1)
    for j in range(4):
        rows, packs = head_rows(j), head_rows(j, AUG)
        keys_t = beside(k4_ref[rows], k4f_ref[rows])
        keys = stack(keys_t, beside(table, table)).T
        values = stack(beside(v4_ref[rows], v4f_ref[rows]), value_rows(HALF)).T
        grads = g2_ref[packs]
        queries = stack(q2_ref[rows], grads[HD:] + qt_ref[...])
        dq, dk4, dv4 = back_block(keys, values, keys_t, queries, q2_ref[rows], grads)
        dq2_ref[rows] = dq.astype(BF)
        keys_t = beside(k8_ref[rows], k8f_ref[rows])
        keys = stack(keys_t, plain).T
        values = stack(beside(v8_ref[rows], v8f_ref[rows]), value_rows(QUARTER)).T
        grads = beside(g3a_ref[packs], g3b_ref[packs])
        plain_q = beside(q3a_ref[rows], q3b_ref[rows])
        queries = stack(plain_q, grads[HD:])
        dq, dk8, dv8 = back_block(keys, values, keys_t, queries, plain_q, grads)
        dq3a_ref[rows] = dq[:, :EIGHTH].astype(BF)
        dq3b_ref[rows] = dq[:, EIGHTH:].astype(BF)
        for kind, own_ref, one_ref, four, eight in (
            (0, dk_ref, dk1_ref, dk4, dk8),
            (1, dv_ref, dv1_ref, dv4, dv8),
        ):
            near, away = eight[:, :EIGHTH], eight[:, EIGHTH:]
            own_ref[rows] = four[:, :QUARTER] + jnp.where(inside, beside(near, near), 0.0)
            extra = four[:, QUARTER:] + jnp.where(inside, beside(away, away), 0.0)
            far_ref[kind, rows] = (one_ref[rows] + extra).astype(BF)


def back0_kernel(*refs):
    q_ref, g_ref, k_ref, v_ref, kt_ref, qt_ref = refs[:6]
    dq_ref, dk_ref, dv_ref = refs[-3:]
    keys_t = k_ref[...]
    keys = stack(keys_t, kt_ref[...]).T
    values = stack(v_ref[...], value_rows(TILES)).T
    block = 512
    dk = dv = None
    for i in range(TILES // block):
        cut = slice(i * block, (i + 1) * block)
        grads = g_ref[:, cut]
        plain_q = q_ref[:, cut]
        queries = stack(plain_q, grads[HD:] + qt_ref[:, cut])
        dq, more_k, more_v = back_block(keys, values, keys_t, queries, plain_q, grads)
        dq_ref[:, cut] = dq.astype(BF)
        dk = more_k if dk is None else dk + more_k
        dv = more_v if dv is None else dv + more_v
    dk_ref[...] = dk.astype(BF)
    dv_ref[...] = dv.astype(BF)


def back_pair(qkv, grads, kv4, kvr, key_table, query_table):
    pair = rows_of(2 * HD, QUARTER)
    pair_v = rows_of(2 * HD, QUARTER, None, HEADS // 2)
    even = lambda height: pl.BlockSpec((height, HALF), lambda i: (2 * i, 0))
    odd = lambda height: pl.BlockSpec((height, HALF), lambda i: (2 * i + 1, 1))
    return pl.pallas_call(
        back1_kernel,
        grid=(HEADS // 2,),
        in_specs=[
            even(HD), odd(HD), even(AUG), odd(AUG), pair, pair_v, pair, pair_v,
            table_spec(HALF, lambda i: i & 3), table_spec(HALF, lambda i: i & 3),
        ],
        out_specs=[
            rows_of(2 * HD, HALF), rows_of(2 * HD, QUARTER), rows_of(2 * HD, QUARTER),
            pl.BlockSpec((2, 2 * HD, QUARTER), lambda i: (0, i, 0)),
        ],
        out_shape=[
            shaped(D, HALF, F32), shaped(D, QUARTER, F32), shaped(D, QUARTER, F32),
            jax.ShapeDtypeStruct((2, D, QUARTER), BF),
        ],
        name="back_pair",
        compiler_params=params(12),
        cost_estimate=cost(PAIRS // 4 * 900, 12 * MIB, PAIRS // 4),
    )(qkv, qkv, grads, grads, kv4, kv4, kvr, kvr, key_table, query_table)


def back_sent(q2, q3a, q3b, g2, g3a, g3b, own, far, tables, dk1, dv1):
    quarter, eighth = rows_of(4 * HD, QUARTER), rows_of(4 * HD, EIGHTH)
    return pl.pallas_call(
        back23_kernel,
        grid=(FOUR,),
        in_specs=[
            quarter, eighth, eighth,
            rows_of(4 * AUG, QUARTER), rows_of(4 * AUG, EIGHTH), rows_of(4 * AUG, EIGHTH), *NEAR,
            table_spec(QUARTER, lambda i: i & 1), table_spec(QUARTER, lambda i: i & 1), quarter, quarter,
        ],
        out_specs=[
            quarter, eighth, eighth, quarter, quarter,
            pl.BlockSpec((2, 4 * HD, QUARTER), lambda i: (0, i, 0)),
        ],
        out_shape=[
            shaped(D, QUARTER, BF), shaped(D, EIGHTH, BF), shaped(D, EIGHTH, BF),
            shaped(D, QUARTER, F32), shaped(D, QUARTER, F32),
            jax.ShapeDtypeStruct((2, D, QUARTER), BF),
        ],
        name="back_sent",
        compiler_params=params(16),
        cost_estimate=cost(PAIRS * 3 // 16 * 900, 12 * MIB, PAIRS * 3 // 16),
    )(q2, q3a, q3b, g2, g3a, g3b, *near_args(own, far), *tables, dk1, dv1)


def back_own(qkv, grads, tables, first, count, before=()):
    full = rows_of(HD, TILES, None, first)
    table = table_spec(TILES, lambda i: (i + first) & 7)
    anywhere = pl.BlockSpec(memory_space=pl.ANY)
    return pl.pallas_call(
        back0_kernel,
        grid=(count,),
        in_specs=[
            full, rows_of(AUG, TILES, None, first), rows_of(HD, TILES, None, HEADS + first),
            rows_of(HD, TILES, None, 2 * HEADS + first), table, table,
        ] + [anywhere] * len(before),
        out_specs=[full, full, full],
        out_shape=[shaped(D, TILES, BF)] * 3,
        input_output_aliases={6 + i: i for i in range(len(before))},
        name="back_own",
        compiler_params=params(16),
        cost_estimate=cost(PAIRS // HEADS * count * 900, 7 * MIB, PAIRS // HEADS * count),
    )(qkv, grads, qkv, qkv, *tables, *before)


def collect_kernel(
    dq_ref, dk_ref, dv_ref, dq1_ref, dq2_ref, dq3a_ref, dq3b_ref, dk4_ref, dv4_ref, far_ref, farr_ref,
    normed_ref, w_ref, grad_ref, back_ref, value_ref,
):
    step = pl.program_id(0)

    def write(base_ref, parts):
        for j in range(GROUP):
            rows = head_rows(j)
            pieces = {
                first: base_ref[rows, first : first + EIGHTH].astype(F32)
                for first in range(0, TILES, EIGHTH)
            }
            for ref, first, count in parts(j):
                for k in range(0, count, EIGHTH):
                    pieces[first + k] = pieces[first + k] + ref[rows, k : k + EIGHTH].astype(F32)
            value_ref[rows] = beside(*(pieces[first] for first in range(0, TILES, EIGHTH))).astype(BF)

    @pl.when(step < GROUPS)
    def _():
        write(
            dq_ref,
            lambda j: (
                (dq1_ref, lanes2(j), HALF), (dq2_ref, lanes4(j), QUARTER),
                (dq3a_ref, lanes8(j), EIGHTH), (dq3b_ref, lanes8(j), EIGHTH),
            ),
        )

    for kind, base_ref, own_ref in ((1, dk_ref, dk4_ref), (2, dv_ref, dv4_ref)):

        @pl.when((step >= kind * GROUPS) & (step < (kind + 1) * GROUPS))
        def _(base_ref=base_ref, own_ref=own_ref):
            write(
                base_ref,
                lambda j: (
                    (own_ref, lanes4(j), QUARTER), (far_ref.at[0], lanes4(j), QUARTER),
                    (farr_ref.at[0], rest2(j), QUARTER),
                ),
            )

    value = value_ref[...]
    grad_ref[...] = nt(normed_ref[...], value).astype(BF)
    back = nn(w_ref[...], value)

    @pl.when(step == 0)
    def _():
        back_ref[...] = back

    @pl.when(step > 0)
    def _():
        back_ref[...] += back


def collect(own, dq1, dq2, dq3a, dq3b, dk4, dv4, far, far_rest, normed, weight):
    def block(width, kind):
        return pl.BlockSpec((ROWS, width), lambda i: (jnp.clip(i - kind * GROUPS, 0, GROUPS - 1), 0))

    away = pl.BlockSpec(
        (1, ROWS, QUARTER),
        lambda i: (jnp.where(i < 2 * GROUPS, 0, 1), jnp.where(i < GROUPS, 0, lax.rem(i, GROUPS)), 0),
    )
    return pl.pallas_call(
        collect_kernel,
        grid=(3 * GROUPS,),
        in_specs=[
            block(TILES, 0), block(TILES, 1), block(TILES, 2),
            block(HALF, 0), block(QUARTER, 0), block(EIGHTH, 0), block(EIGHTH, 0),
            block(QUARTER, 1), block(QUARTER, 2), away, away,
            once(D, TILES), pl.BlockSpec((D, ROWS), lambda i: (0, i)),
        ],
        out_specs=[pl.BlockSpec((D, ROWS), lambda i: (0, i)), whole(D, TILES)],
        out_shape=[shaped(D, 3 * D, BF), shaped(D, TILES, F32)],
        scratch_shapes=[pltpu.VMEM((ROWS, TILES), BF)],
        name="collect",
        compiler_params=params(26),
        cost_estimate=cost(3 * D * TILES * D * 2, 24 * MIB),
    )(*own, dq1, dq2, dq3a, dq3b, dk4, dv4, far, far_rest, normed, weight)


SMALL = 16


def finish_kernel(
    back_ref, order_ref, start_ref, mask_ref, mid_ref, gain_ref,
    masks_ref, feed_ref, up_ref, square_ref, out_ref, small_ref, sums,
):
    step = pl.program_id(0)
    back = nt(order_ref[...], back_ref[...].astype(BF))
    hidden = column(mask_ref[...].astype(F32), D) > 0.5
    hat, scale = normalise(start_ref[...].astype(F32))
    hat_grad = back * as_row(gain_ref)
    first = jnp.mean(hat_grad, axis=1, keepdims=True)
    second = jnp.mean(hat_grad * hat, axis=1, keepdims=True)
    grad = mid_ref[...] + scale * (hat_grad - first - hat * second)
    out_ref[...] = jnp.where(hidden, 0.0, grad).astype(BF)
    more = stack(
        total_rows(back * hat), total_rows(back), total_rows(jnp.where(hidden, grad, 0.0)),
        jnp.zeros((5, D), F32),
    )

    @pl.when(step == 0)
    def _():
        sums[...] = more

    @pl.when(step > 0)
    def _():
        sums[...] += more

    @pl.when(step == pl.num_programs(0) - 1)
    def _():
        width = small_ref.shape[1]
        up = [up_ref[0:1, k * D : (k + 1) * D] for k in range(up_ref.shape[1] // D)]
        rows = stack(sums[0:3], feed_ref[0:6], square_ref[0:1], *up)
        rows = beside(rows, jnp.zeros((rows.shape[0], width - D), F32))
        visible = beside(1.0 - masks_ref[...].astype(F32), jnp.zeros((1, width - TILES), F32))
        rest = jnp.zeros((SMALL - 1 - rows.shape[0], width), F32)
        small_ref[...] = stack(rows, visible, rest).astype(BF)


def finish(back, order, start, mask_row, mid, gain, feed_sums, up_sums, squares):
    block = 256
    ff = up_sums.shape[1]
    part = lambda width: pl.BlockSpec((block, width), lambda i: (i, 0))
    return pl.pallas_call(
        finish_kernel,
        grid=(TILES // block,),
        in_specs=[
            whole(D, TILES), part(TILES), part(D),
            pl.BlockSpec((1, block), lambda i: (0, i)), part(D), line(D),
            whole(1, TILES), whole(8, D), whole(8, ff), whole(8, D),
        ],
        out_specs=[part(D), whole(SMALL, 4 * D)],
        out_shape=[shaped(TILES, D, BF), shaped(SMALL, 4 * D, BF)],
        scratch_shapes=[pltpu.VMEM((8, D), F32)],
        name="finish",
        compiler_params=params(20),
        cost_estimate=cost(TILES * TILES * D, 16 * MIB),
    )(back, order, start, mask_row, mid, gain, mask_row, feed_sums, up_sums, squares)


def exchange(value, axis, mask):
    pairs = [(source, source ^ mask) for source in range(lax.axis_size(axis))]
    return lax.ppermute(value, axis, pairs)


def after(value, *others):
    return lax.optimization_barrier((value,) + others)[0]


def after_all(values, *others):
    return lax.optimization_barrier(tuple(values) + others)[: len(values)]


def swap(value, masks):
    names = tuple(name for name in ("seq", "dp") if name in masks)
    sizes = [lax.axis_size(name) for name in names]

    def partner(index):
        place = []
        for size in reversed(sizes):
            place.append(index % size)
            index //= size
        target = 0
        for size, name, at in zip(sizes, names, reversed(place)):
            target = target * size + (at ^ masks[name])
        return target

    count = int(np.prod(sizes))
    return lax.ppermute(value, names, [(source, partner(source)) for source in range(count)])


def choices(moves):
    for way in range(1, 1 << len(moves)):
        masks = {}
        for k, (axis, bit, _) in enumerate(moves):
            masks.setdefault(axis, 0)
            masks[axis] |= (way >> k & 1) << bit
        yield way, masks


def scatter(value, *moves, plus=None):
    def part(way):
        piece = value
        for k, (axis, bit, dim) in enumerate(moves):
            half = value.shape[dim] // 2
            mine = (lax.axis_index(axis) >> bit & 1) ^ (way >> k & 1)
            piece = lax.dynamic_slice_in_dim(piece, mine * half, half, dim)
        return piece

    pieces = [part(0)] + [swap(part(way), masks) for way, masks in choices(moves)]
    total = pieces[0].astype(F32)
    if plus is not None:
        total = total + plus
    for piece in pieces[1:]:
        total = total + piece.astype(F32)
    return total.astype(BF)


def gather(value, *moves):
    pieces = [value] + [swap(value, masks) for _, masks in choices(moves)]
    stacked = jnp.stack(pieces)
    mine = sum((lax.axis_index(axis) >> bit & 1) << k for k, (axis, bit, _) in enumerate(moves))
    count = len(moves)
    ordered = []
    for place in range(1 << count):
        way = sum((place >> (count - 1 - k) & 1) << k for k in range(count)) ^ mine
        ordered.append(lax.dynamic_index_in_dim(stacked, way, 0, keepdims=False))
    return jnp.concatenate(ordered, axis=0)


def log2_size(axis):
    return (lax.axis_size(axis) - 1).bit_length()


def core_step(value):
    return scatter(value, ("dp", 0, value.ndim - 2))


def near_step(value):
    return scatter(value, ("dp", 1, value.ndim - 2), ("seq", 0, log2_size("seq") - 1))


def far_step(value, zero):
    count = log2_size("seq")
    bits = list(reversed(range(1, count)))
    while bits:
        plus = zero if len(bits) <= 2 else None
        value = scatter(value, *(("seq", bit, count - 1 - bit) for bit in bits[:2]), plus=plus)
        bits = bits[2:]
    return value.reshape(value.shape[-2:])


def in_blocks(grad):
    count = lax.axis_size("seq")
    return grad.reshape((2,) * log2_size("seq") + (grad.shape[0] // count, -1))


def local(
    tokens, tile_mask, cotangent, qkv_weight, proj_weight, proj_bias, up_weight, up_bias,
    down_weight, down_bias, attn_gain, attn_shift, mlp_gain, mlp_shift, mask_vector,
):
    order = order_matrix()
    tables0 = weight_tables(0)
    query_table1 = weight_tables(1)[1]
    key_table1 = weight_tables(1, True)[0]
    tables2 = weight_tables(2)
    seq_count = lax.axis_size("seq")

    normed_t, start, token_squares, qkv, q4, q8, kv4, kvr = embed(
        tokens[0], tile_mask, mask_vector, attn_gain, attn_shift, qkv_weight, order
    )
    q2 = exchange(q4, "seq", 2)
    q3a = exchange(q8, "seq", 4)
    q3b = exchange(q8, "seq", 6)
    kv4_far = exchange(kv4, "seq", 1)
    kvr_far = exchange(after(kvr, kv4_far), "seq", 1)
    own = forward_own(qkv, tables0, 0)
    z2, z3a, z3b = forward_sent(q2, q3a, q3b, kv4, kv4_far, after_all(tables2, own[1]))
    later = after_all(tables0, z2)
    z2 = exchange(z2, "seq", 2)
    z3a = exchange(z3a, "seq", 4)
    z3b = exchange(z3b, "seq", 6)
    own = forward_own(qkv, later, 1, own)
    out1, total1 = forward_pair(qkv, kv4_far, kvr_far, after(key_table1, own[1]), query_table1)
    attn_t, rest, total = merge(*own, out1, total1, z2, z3a, z3b)

    layer_out, grad_mid, grads, g4, g8, feed_sums, up_sums, proj_grad, early = feed(
        order, attn_t, rest, total, start, tile_mask, cotangent[0],
        (proj_bias, down_bias, mlp_gain, mlp_shift, up_bias), proj_weight, up_weight, down_weight,
    )
    early = lax.psum_scatter(early, ("seq", "dp"), scatter_dimension=0, tiled=True)
    g2 = exchange(g4, "seq", 2)
    g3a = exchange(g8, "seq", 4)
    g3b = exchange(g8, "seq", 6)
    dq1, dk1, dv1, far_rest = back_pair(qkv, grads, kv4_far, kvr_far, key_table1, query_table1)
    later = after_all(tables0, far_rest)
    far_rest = exchange(far_rest, "seq", 1)
    part = GROUP // 2
    own_a = back_own(qkv, grads, later, 0, part)
    dq2, dq3a, dq3b, dk4, dv4, far = back_sent(
        q2, q3a, q3b, g2, g3a, g3b, kv4, kv4_far, after_all(tables2, own_a[0]), dk1, dv1
    )
    later = after_all(tables0, far)
    far = exchange(far, "seq", 1)
    dq2 = exchange(dq2, "seq", 2)
    dq3a = exchange(dq3a, "seq", 4)
    dq3b = exchange(dq3b, "seq", 6)
    own = back_own(qkv, grads, later, part, HEADS - part, own_a)
    qkv_grad, back = collect(own, dq1, dq2, dq3a, dq3b, dk4, dv4, far, far_rest, normed_t, qkv_weight)
    chain = in_blocks(qkv_grad)
    seq_dims = chain.shape[:-2]
    chain = jnp.concatenate([core_step(chain), core_step(in_blocks(proj_grad))], axis=-1)
    tokens_grad, small = finish(
        back, order, start, tile_mask, grad_mid, attn_gain, feed_sums, up_sums, token_squares
    )

    share = D // seq_count
    ff = up_weight.shape[1]
    chain = near_step(chain)
    small = near_step(core_step(jnp.broadcast_to(small, seq_dims + small.shape)))
    dp_moves = (("dp", 0, 0), ("dp", 1, 0))
    chain = far_step(jnp.concatenate([chain, small], axis=-2), early[0, 0].astype(F32) * 0.0)
    both = gather(chain, *dp_moves)
    early = gather(early, *reversed(dp_moves))
    quarter, inner = share // 4, chain.shape[0]
    qkv_grad, small = (
        jnp.concatenate([both[k * inner + first : k * inner + last] for k in range(4)])
        for first, last in ((0, quarter), (quarter, inner))
    )
    qkv_grad = qkv_grad.astype(F32)
    qkv_grad, proj_grad = qkv_grad[:, : 3 * D], qkv_grad[:, 3 * D :]
    small = small.astype(F32)
    mine = lax.axis_index("seq") * share
    vectors = lax.dynamic_slice_in_dim(small[:7, :D], mine, share, 1)
    gain_grad, shift_grad, mask_grad, proj_bias_grad, down_bias_grad, gain2_grad, shift2_grad = (
        vectors[k] for k in range(7)
    )
    first = 10
    last = first + ff // D
    up_bias_grad = lax.dynamic_slice_in_dim(
        small[first:last, :D].reshape(ff), lax.axis_index("seq") * (ff // seq_count), ff // seq_count
    )
    middle_squares, final_squares, token_squares, count = (
        jnp.sum(small[k]) for k in (7, 8, 9, last)
    )
    stream_rms = jnp.sqrt(jnp.stack([token_squares, middle_squares, final_squares]) / (count * D))
    early = early.astype(F32)
    up_grad = early[:, :ff]
    down_grad = early[:, ff:].reshape(-1, D)
    return (
        layer_out[None], tokens_grad[None], qkv_grad, proj_grad, proj_bias_grad, up_grad, up_bias_grad,
        down_grad, down_bias_grad, gain_grad, shift_grad, gain2_grad, shift2_grad, mask_grad, stream_rms,
    )


def solution(mesh):
    rows = P("dp", "seq", None)
    in_specs = (rows, P("dp", "seq"), rows) + (P(),) * 12
    matrix, vector = P("seq", None), P("seq")
    out_specs = (
        rows, rows, matrix, matrix, vector, matrix, vector, matrix,
        vector, vector, vector, vector, vector, vector, P(),
    )
    return jax.shard_map(local, mesh=mesh, in_specs=in_specs, out_specs=out_specs, check_vma=False)
```
